512 devices in a mesh: slab: 16 (over x, z_hi), tile: 32 (over z_lo, y, core).
Axes of the slice: x: 4, y: 8, z: 8 (z_hi: 4, z_lo: 2; z = z_hi * 2 + z_lo), core: 2. Of those that a mesh axis runs over, the one named last changes fastest.
Arguments:
- embed: bfloat16 [16, 64, 128, 128], P('slab', 'tile'), may hold values from -12 to 12
- tissue: int32 [16, 64, 128], P('slab', 'tile'), may hold values 0 or 1
- whiten0: bfloat16 [64, 128, 128], replicated, may hold values from -0.2 to 1.2, as said below
- means0: float32 [64, 128], replicated, may hold values from -0.3 to 0.3
- weights0: float32 [64], replicated, may hold values from 1 to 4
Outputs:
- resp_final: float32 [64, 16, 64, 128], P(None, 'slab', 'tile')
- new_means: float32 [64, 128], P('tile')
- score: float32 [], replicated
The draws below stay inside these ranges and needn't reach their ends.
Inputs may be any that keep to these rules, and one draw needn't show every extreme that they name: `whiten0`: every whitening matrix is lower triangular with a positive diagonal.
All inputs are finite; a program needn't handle non-finite values. No bound on the sum of `tissue` on one device may be relied on, other than what follows from the above.
Results may differ from the reference program's by a relative error of at most 0.015.
The reference program's roundings to bfloat16 on the way (of `weighted`) count: a program that leaves them out, or rounds other values in their place, can miss the bound.
Values sent between devices are 32-bit elements; how exact they have to be, the bound alone decides.
No kernel may reach another device: no remote copies, remote signals or barrier semaphores. Data moves between devices by JAX's collectives and lax.ppermute only.
A program may use at most 128 MiB of HBM per device.

```python
import math
import jax
import jax.numpy as jnp
from jax import lax

D = 128
K = 64
SWEEPS = 2
NZ = 16
NY = 64
NX = 128


def draw_whiten0(key, part):
    key = jax.random.fold_in(key, 11)
    diag_key, lower_key = jax.random.split(key)
    diagonal_part = jnp.exp(jax.random.uniform(diag_key, (K, D), minval=-0.05, maxval=0.05))
    lower_part = 0.02 * jax.random.truncated_normal(lower_key, -5.0, 5.0, (K, D, D))
    strict = jnp.tril(lower_part, -1)
    return (strict + diagonal_part[:, :, None] * jnp.eye(D, dtype=jnp.float32)).astype(jnp.bfloat16)


def place_fraction():
    sections = jnp.arange(NZ, dtype=jnp.float32)[:, None]
    rows = jnp.arange(NY, dtype=jnp.float32)[None, :]
    return (sections * NY + rows) / (NZ * NY - 1.0)


def draw_embed(key, part):
    key = jax.random.fold_in(key, 17)
    frac = place_fraction()[:, :, None, None]
    noise = jax.random.truncated_normal(key, -4.0, 4.0, (NZ, NY, NX, D))
    return (noise * (1.0 + 2.0 * frac)).astype(jnp.bfloat16)


def touch_ends(result, key, smallest, largest):
    longest = result.shape.index(max(result.shape))
    spots = []
    for shift in (0, 1):
        where = [jax.random.randint(jax.random.fold_in(key, axis), (), 0, length) for axis, length in enumerate(result.shape)]
        where[longest] = (where[longest] + shift) % result.shape[longest]
        spots.append(tuple(where))
    return result.at[spots[0]].set(smallest).at[spots[1]].set(largest)


def scatter_about(own_key, shape, scale, limit, kind=jnp.bfloat16):
    result = scale * jax.random.normal(own_key, shape, jnp.float32)
    return jnp.clip(result, min=-limit, max=limit).astype(kind)


def setup_inputs(seed: int = 0) -> dict:
    arg_keys = jax.random.split(jax.random.key(seed), 6)
    embed = draw_embed(jax.random.fold_in(arg_keys[5], 71), 0)
    tissue = touch_ends((jax.random.randint(arg_keys[1], (NZ, NY, NX), 0, 5) < 4).astype(jnp.int32), jax.random.fold_in(arg_keys[1], 1), 0, 1)
    whiten0 = draw_whiten0(jax.random.fold_in(arg_keys[5], 71), 0)
    means0 = scatter_about(arg_keys[3], (K, D), 0.05, 0.3, jnp.float32)
    weights0 = jnp.clip(jnp.exp(jax.random.uniform(arg_keys[4], (K,), jnp.float32, math.log(1.0), math.log(4.0))), 1.0, 4.0)
    return dict(embed=embed, tissue=tissue, whiten0=whiten0, means0=means0, weights0=weights0)


BETA_POTTS = 1.0
COV_RIDGE = 0.01

def normalise(scores):
    top = jnp.max(scores, axis=0, keepdims=True)
    expon = jnp.exp(scores - top)
    return expon / jnp.sum(expon, axis=0, keepdims=True)

def neighbour_sum(resp):
    padded = jnp.pad(resp, ((0, 0), (1, 1), (1, 1), (1, 1)))
    total = padded[:, 2:, 1:-1, 1:-1] + padded[:, :-2, 1:-1, 1:-1]
    total = total + padded[:, 1:-1, 2:, 1:-1] + padded[:, 1:-1, :-2, 1:-1]
    total = total + padded[:, 1:-1, 1:-1, 2:] + padded[:, 1:-1, 1:-1, :-2]
    return total

def likelihood(flat, whiten_half, shift, offset):

    def per_domain(pair):
        matrix, centre = pair
        proj = jnp.dot(flat.astype(jnp.float32), matrix.T.astype(jnp.float32), preferred_element_type=jnp.float32) - centre[None, :]
        return jnp.sum(proj * proj, axis=1)
    quad = lax.map(per_domain, (whiten_half, shift))
    return offset[:, None] - 0.5 * quad

def mean_field(scores, tissue_f):
    resp = normalise(scores) * tissue_f[None]
    for sweep in range(SWEEPS):
        resp = normalise(scores + BETA_POTTS * neighbour_sum(resp)) * tissue_f[None]
    return resp

def factor(second, first_moment, counts):
    centre = first_moment / counts[:, None]
    ident = jnp.eye(second.shape[1], dtype=jnp.float32)
    sym = 0.5 * (second + jnp.swapaxes(second, 1, 2))
    cov = sym / counts[:, None, None] - centre[:, :, None] * centre[:, None, :] + COV_RIDGE * ident
    lower = jnp.linalg.cholesky(cov)

    def solve_one(lower_one):
        return jax.scipy.linalg.solve_triangular(lower_one, ident, lower=True)
    whiten = jax.vmap(solve_one)(lower)
    logdet = -jnp.sum(jnp.log(jnp.diagonal(lower, axis1=1, axis2=2)), axis=1)
    return (whiten, logdet)

def offsets(whiten_full, centre, logdet, counts):
    shift = jnp.einsum('kde,ke->kd', whiten_full, centre, precision=lax.Precision.HIGHEST)
    return (shift, jnp.log(counts / jnp.sum(counts)) + logdet)

def reference(embed, tissue, whiten0, means0, weights0):
    flat = embed.reshape(-1, D)
    tissue_f = tissue.astype(jnp.float32)
    start_full = whiten0.astype(jnp.float32)
    logdet0 = jnp.sum(jnp.log(jnp.diagonal(start_full, axis1=1, axis2=2)), axis=1)
    shift0, offset0 = offsets(start_full, means0, logdet0, weights0)
    grid = (K, NZ, NY, NX)
    resp = mean_field(likelihood(flat, whiten0, shift0, offset0).reshape(grid), tissue_f)
    flat_resp = resp.reshape(K, -1)

    def moments(weights_row):
        weighted = (weights_row[:, None] * flat.astype(jnp.float32)).astype(jnp.bfloat16)
        second_one = jnp.dot(weighted.T.astype(jnp.float32), flat.astype(jnp.float32), preferred_element_type=jnp.float32)
        return (second_one, jnp.sum(weighted.astype(jnp.float32), axis=0))
    second, first_moment = lax.map(moments, flat_resp)
    counts = jnp.sum(flat_resp, axis=1)
    centre = first_moment / counts[:, None]
    whiten, logdet = factor(second, first_moment, counts)
    shift, offset = offsets(whiten, centre, logdet, counts)
    scores = likelihood(flat, whiten.astype(jnp.bfloat16), shift, offset)
    top = jnp.max(scores, axis=0)
    lse = top + jnp.log(jnp.sum(jnp.exp(scores - top[None]), axis=0))
    score = jnp.sum(lse * tissue_f.reshape(-1)) / (NZ * NY * NX)
    resp_final = mean_field(scores.reshape(grid), tissue_f)
    return (resp_final, centre, score)
```

```python
import jax
import jax.numpy as jnp
from jax import lax
from jax.experimental import pallas as pl
from jax.experimental.pallas import tpu as pltpu
from jax.sharding import Mesh
from jax.sharding import PartitionSpec as P

SWEEPS = 2
BETA_POTTS = 1.0
COV_RIDGE = 0.01

SLAB = ("x1", "x0", "z2", "z1")
TILE = ("z0", "y2", "y1", "y0", "core")
BRICK = ("z0", "y0", "core")
PAIRS = ("x0", "y1")
ROWS = ("x1", "z2", "z1", "y2")

WIDTH = 128
CELLS = 256
PACKET = 144
HIGH = lax.Precision.HIGHEST
VMEM = pl.BlockSpec(memory_space=pltpu.VMEM)
PARAMS = pltpu.CompilerParams(vmem_limit_bytes=40 * 1024 * 1024)


def call(kernel, shapes, *args, flops=1 << 20):
    out = [jax.ShapeDtypeStruct(shape, kind) for shape, kind in shapes]
    return pl.pallas_call(
        kernel,
        out_shape=out,
        in_specs=[VMEM] * len(args),
        out_specs=[VMEM] * len(out),
        compiler_params=PARAMS,
        cost_estimate=pl.CostEstimate(flops=flops, bytes_accessed=1 << 20, transcendentals=0),
    )(*args)


def iotas(shape):
    return (
        lax.broadcasted_iota(jnp.int32, shape, 0),
        lax.broadcasted_iota(jnp.int32, shape, 1),
    )


def matmul(lhs, rhs, dims=((1,), (0,)), precision=None):
    return lax.dot_general(
        lhs, rhs, (dims, ((), ())), precision=precision, preferred_element_type=jnp.float32
    )


def normalise(scores):
    top = jnp.max(scores, axis=0, keepdims=True)
    expon = jnp.exp(scores - top)
    return expon / jnp.sum(expon, axis=0, keepdims=True)


def put(resp, resp_ref, first_ref, last_ref):
    resp_ref[...] = resp
    first_ref[...] = resp[:, :WIDTH]
    last_ref[...] = resp[:, WIDTH:]


def domain_at(place):
    bit = lambda n: (place >> n) & 1
    return bit(5) * 32 + bit(2) * 16 + bit(1) * 8 + bit(4) * 4 + bit(3) * 2 + bit(0)


def start_kernel(flat, tissue, whiten, means, weights, scores, resp, first, last, diag, weigh):
    turned = flat[...].astype(jnp.float32).T.astype(jnp.bfloat16)
    row_at, col_at = iotas((WIDTH, WIDTH))
    count = whiten.shape[0]

    def domain(place, carry):
        own = domain_at(place)
        matrix = whiten[own]
        full = matrix.astype(jnp.float32)
        shift = jnp.sum(full * means[pl.ds(own, 1), :], axis=1, keepdims=True)
        proj = matmul(matrix, turned) - shift
        scores[pl.ds(place, 1), :] = jnp.sum(proj * proj, axis=0, keepdims=True)
        diag[pl.ds(place, 1), :] = jnp.sum(
            jnp.where(row_at == col_at, full, 0.0), axis=0, keepdims=True
        )
        weigh[pl.ds(place, 1), :] = weights[pl.ds(own, 1), :]
        return carry

    lax.fori_loop(0, count, domain, 0, unroll=4)
    total = jnp.sum(weigh[...], axis=0, keepdims=True)
    offset = jnp.log(weigh[...] / total) + jnp.sum(jnp.log(diag[...]), axis=1, keepdims=True)
    result = offset[:, :1] - 0.5 * scores[...]
    scores[...] = result
    put(normalise(result) * tissue[...], resp, first, last)


def start(flat, tissue, whiten, means, weights):
    count = whiten.shape[0]
    f32 = jnp.float32
    return pl.pallas_call(
        start_kernel,
        out_shape=[
            jax.ShapeDtypeStruct((count, CELLS), f32),
            jax.ShapeDtypeStruct((count, CELLS), f32),
            jax.ShapeDtypeStruct((count, WIDTH), f32),
            jax.ShapeDtypeStruct((count, WIDTH), f32),
        ],
        in_specs=[VMEM] * 5,
        out_specs=[VMEM] * 4,
        scratch_shapes=[pltpu.VMEM((count, WIDTH), f32), pltpu.VMEM((count, WIDTH), f32)],
        compiler_params=PARAMS,
        cost_estimate=pl.CostEstimate(flops=1 << 29, bytes_accessed=1 << 21, transcendentals=0),
    )(flat, tissue, whiten, means, weights)


def sweep_kernel(scores, resp, ahead, behind, below, above, tissue, out, first, last):
    lane = iotas((resp.shape[0], WIDTH))[1]
    rows = (resp[:, :WIDTH], resp[:, WIDTH:])
    fields = []
    for row, others in zip(rows, (below[...] + rows[1], rows[0] + above[...])):
        after = jnp.where(lane < WIDTH - 1, pltpu.roll(row, WIDTH - 1, 1), 0.0)
        before = jnp.where(lane > 0, pltpu.roll(row, 1, 1), 0.0)
        fields.append(others + after + before)
    field = jnp.concatenate(fields, axis=1) + ahead[...] + behind[...]
    put(normalise(scores[...] + BETA_POTTS * field) * tissue[...], out, first, last)


def sweep(scores, resp, first, last, tissue):
    def moved(part, axes, step):
        count = lax.axis_size(axes)
        pairs = [(i, i + step) for i in range(count) if 0 <= i + step < count]
        return lax.ppermute(part, axes, pairs)

    f32 = jnp.float32
    below = moved(last, TILE, 1)
    above = moved(first, TILE, -1)
    behind = moved(resp, SLAB, 1)
    ahead = moved(resp, SLAB, -1)
    count = resp.shape[0]
    return call(
        sweep_kernel,
        [((count, CELLS), f32), ((count, WIDTH), f32), ((count, WIDTH), f32)],
        scores, resp, ahead, behind, below, above, tissue,
    )


def moments_kernel(resp, shared, packet, turned, total):
    blocks, count = resp.shape[:2]
    row_at, col_at = iotas((WIDTH, WIDTH))
    ones = jnp.ones((CELLS, WIDTH), jnp.bfloat16)
    acc = [jnp.zeros((WIDTH, 2 * WIDTH), jnp.float32) for _ in range(count)]
    for block in range(blocks):
        cells = shared[block * CELLS : (block + 1) * CELLS, :]
        flipped = cells.T
        turned[block] = flipped.astype(jnp.bfloat16)
        wide = jnp.concatenate([cells.astype(jnp.bfloat16), ones], axis=1)
        for k in range(count):
            weighted = (flipped * resp[block, k : k + 1, :]).astype(jnp.bfloat16)
            acc[k] = acc[k] + matmul(weighted, wide)
    firsts = jnp.zeros((WIDTH, WIDTH), jnp.float32)
    for k in range(count):
        firsts = jnp.where(col_at == k, acc[k][:, WIDTH:], firsts)
    firsts = firsts.T
    counts = jnp.sum(jnp.sum(resp[...], axis=0), axis=1, keepdims=True)
    counts = jnp.broadcast_to(counts, (count, WIDTH))
    total[...] = jnp.sum(counts, axis=0, keepdims=True)
    for pair in range(count // 2):
        a, b = acc[2 * pair][:, :WIDTH], acc[2 * pair + 1][:, :WIDTH]
        crossed = jnp.where(row_at > col_at, b, a).T
        packet[pair, :WIDTH] = jnp.where(row_at >= col_at, a, b) + crossed
        diag = jnp.sum(jnp.where(row_at == col_at, b, 0.0), axis=0, keepdims=True)
        packet[pair, WIDTH:] = jnp.concatenate(
            [
                2.0 * diag,
                firsts[2 * pair : 2 * pair + 2],
                counts[2 * pair : 2 * pair + 2],
                jnp.zeros((PACKET - WIDTH - 5, WIDTH), jnp.float32),
            ],
            axis=0,
        )


STEP = 8


def whiten_chain(cov):
    row_at, col_at = iotas((WIDTH, WIDTH))
    wide = (STEP, 2 * WIDTH)
    rest = jnp.concatenate([cov, jnp.where(row_at == col_at, 1.0, 0.0)], axis=1)
    sub = lax.broadcasted_iota(jnp.int32, (STEP, WIDTH), 0)
    done, scales = [], []
    for begin in range(0, WIDTH, STEP):
        panel = rest[:STEP]
        cols = [
            jnp.broadcast_to(panel[:, begin + j : begin + j + 1], (STEP, WIDTH))
            for j in range(STEP)
        ]
        scale = jnp.broadcast_to(cols[0][:1], (STEP, WIDTH))
        for j in range(STEP - 1):
            pivot = jnp.broadcast_to(cols[j][j : j + 1], (STEP, WIDTH))
            mult = jnp.where(sub > j, cols[j] / pivot, 0.0)
            both = jnp.concatenate([mult, mult], axis=1)
            panel = panel - both * jnp.broadcast_to(panel[j : j + 1], wide)
            for l in range(j + 1, STEP):
                cols[l] = cols[l] - mult * jnp.broadcast_to(cols[l][j : j + 1], (STEP, WIDTH))
            scale = jnp.where(sub > j, jnp.broadcast_to(cols[j + 1][j + 1 : j + 2], (STEP, WIDTH)), scale)
        root = lax.rsqrt(scale)
        panel = panel * jnp.concatenate([root, root], axis=1)
        scales.append(scale)
        done.append(panel[:, WIDTH:])
        if begin + STEP < WIDTH:
            below = panel[:, :WIDTH]
            rest = rest[STEP:] - matmul(below, panel, ((0,), (0,)), HIGH)[begin + STEP :]
    logdet = -0.5 * jnp.sum(jnp.log(jnp.concatenate(scales, axis=0)), axis=0, keepdims=True)
    return jnp.concatenate(done, axis=0), logdet


def factor_kernel(packet, out):
    row_at, col_at = iotas((WIDTH, WIDTH))
    square = packet[:WIDTH]
    turned = square.T
    diag = packet[WIDTH : WIDTH + 1]
    syms = (
        jnp.where(row_at >= col_at, square, turned),
        jnp.where(row_at < col_at, square, jnp.where(row_at == col_at, diag, turned)),
    )
    extras = [jnp.zeros((1, WIDTH), jnp.float32)] * 8
    whitens = []
    for which, sym in enumerate(syms):
        counts = packet[WIDTH + 3 + which : WIDTH + 4 + which]
        centre = packet[WIDTH + 1 + which : WIDTH + 2 + which] / counts
        tall = jnp.broadcast_to(centre, (WIDTH, WIDTH))
        cov = 0.5 * sym / counts - tall.T * tall
        cov = jnp.where(row_at == col_at, cov + COV_RIDGE, cov)
        whiten, logdet = whiten_chain(cov)
        whitens.append(whiten)
        shift = jnp.sum(whiten * tall, axis=1, keepdims=True)
        extras[1 + which] = jnp.broadcast_to(shift, (WIDTH, WIDTH)).T[:1]
        extras[3 + which] = centre
        extras[5 + which] = jnp.log(counts) + logdet
    extras[0] = jnp.sum(jnp.where(row_at == col_at, whitens[1], 0.0), axis=0, keepdims=True)
    out[:WIDTH] = jnp.where(row_at >= col_at, whitens[0], whitens[1].T)
    out[WIDTH:] = jnp.concatenate(extras, axis=0)


def second_kernel(packets, turned, scores):
    row_at, col_at = iotas((WIDTH, WIDTH))
    blocks = turned.shape[0]
    for pair in range(packets.shape[0]):
        square = packets[pair, :WIDTH]
        extras = packets[pair, WIDTH:]
        upper = jnp.where(row_at < col_at, square, 0.0)
        upper = jnp.where(row_at == col_at, extras[:1], upper)
        whitens = (jnp.where(row_at >= col_at, square, 0.0), upper.T)
        for which, whiten in enumerate(whitens):
            half = whiten.astype(jnp.bfloat16)
            shift = jnp.broadcast_to(extras[1 + which : 2 + which], (WIDTH, WIDTH)).T
            shift = jnp.concatenate([shift, shift], axis=1)
            offset = extras[5 + which : 6 + which]
            offset = jnp.concatenate([offset, offset], axis=1)
            for block in range(blocks):
                proj = matmul(half, turned[block]) - shift
                quad = jnp.sum(proj * proj, axis=0, keepdims=True)
                k = 2 * pair + which
                scores[block, k : k + 1, :] = offset - 0.5 * quad


def likely_kernel(scores, tissue, total, resp, first, last, totals):
    values = scores[...]
    top = jnp.max(values, axis=0, keepdims=True)
    expon = jnp.exp(values - top)
    weight = jnp.sum(expon, axis=0, keepdims=True)
    put(expon / weight * tissue[...], resp, first, last)
    lse = jnp.sum((top + jnp.log(weight)) * tissue[...], axis=1, keepdims=True)
    cover = jnp.sum(tissue[...], axis=1, keepdims=True)
    lane = iotas((1, WIDTH))[1]
    totals[...] = jnp.where(lane == 0, lse, jnp.where(lane == 1, cover, total[...]))


def to_all(value, axes):
    count = lax.axis_size(axes)
    spread = jnp.broadcast_to(value[None], (count, *value.shape))
    return lax.all_to_all(spread, axes, 0, 0, tiled=True)


def shards(embed, tissue, whiten0, means0, weights0):
    count = whiten0.shape[0]
    f32 = jnp.float32
    flat = embed.reshape(CELLS, WIDTH)
    tissue_f = tissue.astype(f32).reshape(1, CELLS)

    shared = lax.all_gather(flat.astype(f32), BRICK, axis=0, tiled=True)
    shared = lax.optimization_barrier(shared)

    spread = jnp.broadcast_to(weights0[:, None], (count, WIDTH))
    scores, resp, first, last = start(flat, tissue_f, whiten0, means0, spread)
    for _ in range(SWEEPS):
        resp, first, last = sweep(scores, resp, first, last, tissue_f)

    part = lax.all_to_all(resp.reshape(8, 8, CELLS), BRICK, 0, 0, tiled=True)
    packet, turned, total = call(
        moments_kernel,
        [((4, PACKET, WIDTH), f32), ((8, WIDTH, CELLS), jnp.bfloat16), ((1, WIDTH), f32)],
        part, shared, flops=1 << 30,
    )
    packet = packet.reshape(64, 1, PACKET * WIDTH // 16)
    packet = lax.all_to_all(packet, PAIRS + ROWS, 0, 0, tiled=True)
    packet = to_all(jnp.sum(packet, axis=0), ROWS).reshape(PACKET, WIDTH)

    (own,) = call(factor_kernel, [((WIDTH + 8, WIDTH), f32)], packet, flops=1 << 27)
    packets = to_all(own, PAIRS)
    (part,) = call(second_kernel, [((8, 8, CELLS), f32)], packets, turned, flops=1 << 29)
    scores = lax.all_to_all(part, BRICK, 0, 0, tiled=True).reshape(count, CELLS)

    resp, first, last, totals = call(
        likely_kernel,
        [((count, CELLS), f32), ((count, WIDTH), f32), ((count, WIDTH), f32), ((1, WIDTH), f32)],
        scores, tissue_f, total,
    )
    totals = jnp.sum(to_all(totals, SLAB), axis=0)
    totals = jnp.sum(to_all(totals, TILE), axis=0)
    bins = CELLS * lax.axis_size(SLAB + TILE)
    score = (totals[0, 0] - totals[0, 1] * jnp.log(totals[0, 2])) / bins
    for _ in range(SWEEPS):
        resp, first, last = sweep(scores, resp, first, last, tissue_f)

    resp_final = resp.reshape(2, 2, 2, 2, 2, 2, 1, 2, WIDTH).transpose(0, 3, 4, 1, 2, 5, 6, 7, 8)
    means = packets[:, WIDTH + 3 : WIDTH + 5]
    place = lax.axis_index(("y2", "y1"))
    means_out = lax.dynamic_index_in_dim(means, place, 0, keepdims=False)
    return (resp_final.reshape(count, 1, 2, WIDTH), means_out, score)


def solution(mesh):
    bits = Mesh(mesh.devices.reshape((2,) * 9), SLAB + TILE)
    in_specs = (P(SLAB, TILE, None, None), P(SLAB, TILE, None), P(), P(), P())
    out_specs = (P(None, SLAB, TILE, None), P(TILE, None), P())
    return jax.shard_map(shards, mesh=bits, in_specs=in_specs, out_specs=out_specs, check_vma=False)
```

```python
import jax
import jax.numpy as jnp
from jax import lax
from jax.experimental import pallas as pl
from jax.experimental.pallas import tpu as pltpu
from jax.sharding import Mesh
from jax.sharding import PartitionSpec as P

SWEEPS = 2
BETA_POTTS = 1.0
COV_RIDGE = 0.01

SLAB = ("x1", "x0", "z2", "z1")
TILE = ("z0", "y2", "y1", "y0", "core")
BRICK = ("x1", "x0", "core")
NEAR = ("y2", "y1", "y0")
FAR = ("z2", "z1", "z0")
ROUND = (("y2", "y1", "y0", "core"), ("x1", "x0", "z2", "z1", "z0"))

WIDTH = 128
CELLS = 256
HALF = 64
PACKET = HALF + 8
VMEM = pl.BlockSpec(memory_space=pltpu.VMEM)
SMEM = pl.BlockSpec(memory_space=pltpu.SMEM)
HBM = pl.BlockSpec(memory_space=pl.ANY)
PARAMS = pltpu.CompilerParams(vmem_limit_bytes=40 * 1024 * 1024)


def call(kernel, shapes, *args, scalars=0, flops=1 << 20):
    out = [jax.ShapeDtypeStruct(shape, kind) for shape, kind in shapes]
    return pl.pallas_call(
        kernel,
        out_shape=out,
        in_specs=[SMEM] * scalars + [VMEM] * (len(args) - scalars),
        out_specs=[VMEM] * len(out),
        compiler_params=PARAMS,
        cost_estimate=pl.CostEstimate(flops=flops, bytes_accessed=1 << 20, transcendentals=0),
    )(*args)


def iotas(shape):
    return (
        lax.broadcasted_iota(jnp.int32, shape, 0),
        lax.broadcasted_iota(jnp.int32, shape, 1),
    )


def matmul(lhs, rhs, dims=((1,), (0,))):
    return lax.dot_general(lhs, rhs, (dims, ((), ())), preferred_element_type=jnp.float32)


def normalise(scores):
    top = jnp.max(scores, axis=0, keepdims=True)
    expon = jnp.exp(scores - top)
    return expon / jnp.sum(expon, axis=0, keepdims=True)


def put(core, resp, resp_ref, near_ref, far_ref):
    first, last = resp[:, :WIDTH], resp[:, WIDTH:]
    resp_ref[...] = resp
    near_ref[...] = jnp.where(core == 0, last, first)
    far_ref[...] = jnp.where(core == 0, first, last)


CHUNK = 16


def start_kernel(
    core, weights, flat, tissue, means, whiten,
    scores, resp, near, far, spread, mask,
    weights_in, flat_in, tissue_in, means_in, whiten_in, diag, sems,
):
    count = whiten.shape[0]
    small = zip((flat, means, tissue, weights), (flat_in, means_in, tissue_in, weights_in))
    copies = [pltpu.make_async_copy(src, dst, sems.at[n]) for n, (src, dst) in enumerate(small)]
    blocks = [
        pltpu.make_async_copy(
            whiten.at[pl.ds(begin, CHUNK)],
            whiten_in.at[pl.ds(begin, CHUNK)],
            sems.at[4 + begin // CHUNK],
        )
        for begin in range(0, count, CHUNK)
    ]
    for copy in copies + blocks:
        copy.start()
    row_at, col_at = iotas((WIDTH, WIDTH))
    copies[0].wait()
    full = flat_in[...].astype(jnp.float32)
    cells = full.T.astype(jnp.bfloat16)
    for n in range(spread.shape[0]):
        spread[n] = full
    for copy in copies[1:]:
        copy.wait()
    for n, block in enumerate(blocks):
        block.wait()
        for own in range(n * CHUNK, (n + 1) * CHUNK):
            matrix = whiten_in[own]
            full = matrix.astype(jnp.float32)
            shift = jnp.sum(full * means_in[own : own + 1], axis=1, keepdims=True)
            proj = matmul(matrix, cells) - shift
            scores[own : own + 1] = jnp.sum(proj * proj, axis=0, keepdims=True)
            diag[own : own + 1] = jnp.sum(
                jnp.where(row_at == col_at, full, 0.0), axis=0, keepdims=True
            )
    prior = weights_in[...]
    prior = jnp.log(prior / jnp.sum(prior, axis=1, keepdims=True))
    row_at, col_at = iotas((count, count))
    prior = jnp.where(row_at == col_at, jnp.broadcast_to(prior, (count, count)), 0.0)
    offset = jnp.sum(prior, axis=1, keepdims=True) + jnp.sum(
        jnp.log(diag[...]), axis=1, keepdims=True
    )
    result = offset - 0.5 * scores[...]
    scores[...] = result
    tissue_f = tissue_in[...].astype(jnp.float32)
    tissue_f = jnp.concatenate([tissue_f[:1], tissue_f[1:]], axis=1)
    mask[...] = tissue_f
    put(core[0], normalise(result) * tissue_f, resp, near, far)


def start(core, weights, flat, tissue, means, whiten):
    count = whiten.shape[0]
    f32 = jnp.float32
    shapes = [(count, CELLS), (count, CELLS), (count, WIDTH), (count, WIDTH)]
    shapes += [(8, CELLS, WIDTH), (1, CELLS)]
    return pl.pallas_call(
        start_kernel,
        out_shape=[jax.ShapeDtypeStruct(shape, f32) for shape in shapes],
        in_specs=[SMEM] + [HBM] * 5,
        out_specs=[VMEM] * len(shapes),
        scratch_shapes=[
            pltpu.VMEM(weights.shape, f32),
            pltpu.VMEM(flat.shape, flat.dtype),
            pltpu.VMEM(tissue.shape, tissue.dtype),
            pltpu.VMEM(means.shape, f32),
            pltpu.VMEM(whiten.shape, whiten.dtype),
            pltpu.VMEM((count, WIDTH), f32),
            pltpu.SemaphoreType.DMA((4 + count // CHUNK,)),
        ],
        compiler_params=pltpu.CompilerParams(vmem_limit_bytes=58 * 1024 * 1024),
        cost_estimate=pl.CostEstimate(flops=1 << 29, bytes_accessed=1 << 21, transcendentals=0),
    )(core, weights, flat, tissue, means, whiten)


def sweep_kernel(
    core, scores, resp, slab_even, slab_odd, near_in, far_in, mask, out, near, far
):
    lane = iotas((resp.shape[0], WIDTH))[1]
    rows = (resp[:, :WIDTH], resp[:, WIDTH:])
    below = jnp.where(core[0] == 0, far_in[...], near_in[...])
    above = jnp.where(core[0] == 0, near_in[...], far_in[...])
    fields = []
    for row, others in zip(rows, (below + rows[1], rows[0] + above)):
        after = jnp.where(lane < WIDTH - 1, pltpu.roll(row, WIDTH - 1, 1), 0.0)
        before = jnp.where(lane > 0, pltpu.roll(row, 1, 1), 0.0)
        fields.append(others + after + before)
    field = jnp.concatenate(fields, axis=1) + slab_even[...] + slab_odd[...]
    put(core[0], normalise(scores[...] + BETA_POTTS * field) * mask[...], out, near, far)


def swapped(part, axes, begin):
    count = lax.axis_size(axes)
    pairs = [(i, i + 1) for i in range(begin, count - 1, 2)]
    return lax.ppermute(part, axes, pairs + [(j, i) for i, j in pairs])


def sweep(core, scores, resp, near, far, mask):
    f32 = jnp.float32
    count = resp.shape[0]
    return call(
        sweep_kernel,
        [((count, CELLS), f32), ((count, WIDTH), f32), ((count, WIDTH), f32)],
        core, scores, resp, swapped(resp, SLAB, 0), swapped(resp, SLAB, 1),
        swapped(near, TILE, 0), swapped(far, TILE, 1), mask, scalars=1,
    )


def moments_kernel(resp, shared, packet, turned, total):
    blocks, count = resp.shape[:2]
    row_at, col_at = iotas((WIDTH, WIDTH))
    ones = jnp.ones((CELLS, WIDTH), jnp.bfloat16)
    acc = [jnp.zeros((WIDTH, 2 * WIDTH), jnp.float32) for _ in range(count)]
    for block in range(blocks):
        cells = shared[block]
        flipped = cells.T
        turned[block] = flipped.astype(jnp.bfloat16)
        wide = jnp.concatenate([cells.astype(jnp.bfloat16), ones], axis=1)
        for k in range(count):
            weighted = (flipped * resp[block, k : k + 1, :]).astype(jnp.bfloat16)
            acc[k] = acc[k] + matmul(weighted, wide)
    firsts = jnp.zeros((WIDTH, WIDTH), jnp.float32)
    for k in range(count):
        firsts = jnp.where(col_at == k, acc[k][:, WIDTH:], firsts)
    firsts = firsts.T
    counts = jnp.sum(jnp.sum(resp[...], axis=0), axis=1, keepdims=True)
    counts = jnp.broadcast_to(counts, (count, WIDTH))
    total[...] = jnp.sum(counts, axis=0, keepdims=True)
    fold_row, fold_col = iotas((HALF, WIDTH))
    for k in range(count):
        sym = acc[k][:, :WIDTH]
        sym = sym + sym.T
        low = (fold_col < HALF) | (fold_row > fold_col - HALF)
        packet[k, :HALF] = jnp.where(low, sym[HALF:], pltpu.roll(sym[:HALF], HALF, 1))
        diag = jnp.sum(jnp.where(row_at == col_at, sym, 0.0), axis=0, keepdims=True)
        packet[k, HALF:] = jnp.concatenate(
            [diag, firsts[k : k + 1], counts[k : k + 1], jnp.zeros((5, WIDTH), jnp.float32)],
            axis=0,
        )


def gather_kernel(packets, out):
    total = jnp.sum(packets[...], axis=0)
    for k in range(out.shape[0]):
        out[k] = total


def split(value):
    high = value.astype(jnp.bfloat16).astype(jnp.float32)
    rest = value - high
    middle = rest.astype(jnp.bfloat16).astype(jnp.float32)
    return high, middle, rest - middle


STEP = 16


def whiten_chain(cov):
    row_at, col_at = iotas((WIDTH, WIDTH))
    wide = (STEP, 2 * WIDTH)
    rest = jnp.concatenate([cov, jnp.where(row_at == col_at, 1.0, 0.0)], axis=1)
    sub = lax.broadcasted_iota(jnp.int32, (STEP, WIDTH), 0)
    done, scales = [], []
    for begin in range(0, WIDTH, STEP):
        panel = rest[:STEP]
        cols = [
            jnp.broadcast_to(panel[:, begin + j : begin + j + 1], (STEP, WIDTH))
            for j in range(STEP)
        ]
        scale = jnp.broadcast_to(cols[0][:1], (STEP, WIDTH))
        for j in range(STEP - 1):
            inverse = 1.0 / cols[j][j : j + 1]
            mult = jnp.where(sub > j, cols[j] * inverse, 0.0)
            for l in range(j + 1, STEP):
                cols[l] = cols[l] - mult * jnp.broadcast_to(cols[l][j : j + 1], (STEP, WIDTH))
            both = jnp.concatenate([mult, mult], axis=1)
            panel = panel - both * jnp.broadcast_to(panel[j : j + 1], wide)
            pivot = jnp.broadcast_to(cols[j + 1][j + 1 : j + 2], (STEP, WIDTH))
            scale = jnp.where(sub > j, pivot, scale)
        root = lax.rsqrt(scale)
        panel = panel * jnp.concatenate([root, root], axis=1)
        scales.append(scale)
        done.append(panel[:, WIDTH:])
        if begin + STEP < WIDTH:
            high, middle, low = split(panel)
            right = jnp.concatenate([high, middle, low, high, middle, high], axis=0)
            high, middle, low = (part[:, :WIDTH] for part in (high, middle, low))
            left = jnp.concatenate([high, high, high, middle, middle, low], axis=0)
            update = matmul(left.astype(jnp.bfloat16), right.astype(jnp.bfloat16), ((0,), (0,)))
            rest = rest[STEP:] - update[begin + STEP :]
    logdet = -0.5 * jnp.sum(jnp.log(jnp.concatenate(scales, axis=0)), axis=0, keepdims=True)
    return jnp.concatenate(done, axis=0), logdet


def unfolded(fold):
    both = jnp.concatenate([pltpu.roll(fold, HALF, 1), fold], axis=0)
    return both, both.T


def factor_kernel(packets, out):
    row_at, col_at = iotas((WIDTH, WIDTH))
    packet = jnp.sum(packets[...], axis=0)
    both, turned = unfolded(packet[:HALF])
    diag, first, counts = (packet[HALF + n : HALF + n + 1] for n in range(3))
    left = col_at < HALF
    kept = (left & (row_at <= col_at)) | ((row_at >= HALF) & (left | (row_at > col_at)))
    sym = jnp.where(row_at == col_at, diag, jnp.where(kept, both, turned))
    centre = first / counts
    tall = jnp.broadcast_to(centre, (WIDTH, WIDTH))
    cov = 0.5 * sym / counts - tall.T * tall
    cov = jnp.where(row_at == col_at, cov + COV_RIDGE, cov)
    whiten, logdet = whiten_chain(cov)
    shift = jnp.sum(whiten * tall, axis=1, keepdims=True)
    shift = jnp.broadcast_to(shift, (WIDTH, WIDTH)).T[:1]
    offset = jnp.log(counts) + logdet
    diag = jnp.sum(jnp.where(row_at == col_at, whiten, 0.0), axis=0, keepdims=True)
    fold_row, fold_col = iotas((HALF, WIDTH))
    low = (fold_col < HALF) | (fold_row >= fold_col - HALF)
    fold = jnp.where(low, whiten[HALF:], pltpu.roll(whiten.T[:HALF], HALF, 1))
    zeros = jnp.zeros((4, WIDTH), jnp.float32)
    result = jnp.concatenate([fold, diag, shift, centre, offset, zeros], axis=0)
    for k in range(out.shape[0]):
        out[k] = result


def second_kernel(packets, turned, scores):
    row_at, col_at = iotas((WIDTH, WIDTH))
    top, left = row_at < HALF, col_at < HALF
    below = (row_at >= HALF) & (left | (row_at >= col_at))
    above = top & (row_at > col_at)
    for k in range(packets.shape[0]):
        both, flipped = unfolded(packets[k, :HALF])
        diag, shift, centre, offset = (packets[k, HALF + n : HALF + n + 1] for n in range(4))
        whiten = jnp.where(below, both, jnp.where(above, flipped, 0.0))
        half = jnp.where(top & (row_at == col_at), diag, whiten).astype(jnp.bfloat16)
        shift = jnp.broadcast_to(shift, (WIDTH, WIDTH)).T
        shift = jnp.concatenate([shift, shift], axis=1)
        offset = jnp.concatenate([offset, offset], axis=1)
        for block in range(turned.shape[0]):
            proj = matmul(half, turned[block]) - shift
            quad = jnp.sum(proj * proj, axis=0, keepdims=True)
            scores[block, k : k + 1, :CELLS] = offset - 0.5 * quad
            scores[block, k : k + 1, CELLS:] = centre


def likely_kernel(place, part, mask, total, scores, resp, near, far, means, totals):
    values = part[:, :CELLS]
    scores[...] = values
    row = iotas((part.shape[0], WIDTH))[0]
    for n in range(2):
        own = jnp.where(row == 2 * place[1] + n, part[:, CELLS:], 0.0)
        means[n : n + 1] = jnp.sum(own, axis=0, keepdims=True)
    tissue_f = mask[...]
    top = jnp.max(values, axis=0, keepdims=True)
    expon = jnp.exp(values - top)
    weight = jnp.sum(expon, axis=0, keepdims=True)
    put(place[0], expon / weight * tissue_f, resp, near, far)
    lse = jnp.sum((top + jnp.log(weight)) * tissue_f, axis=1, keepdims=True)
    cells = jnp.sum(tissue_f, axis=1, keepdims=True)
    lane = iotas((1, WIDTH))[1]
    result = jnp.where(lane == 0, lse, jnp.where(lane == 1, cells, total[...]))
    for n in range(totals.shape[0]):
        totals[n] = result


def swap_all(value, axes):
    return lax.all_to_all(value, axes, 0, 0, tiled=True)


def shards(embed, tissue, whiten0, means0, weights0):
    count = whiten0.shape[0]
    f32 = jnp.float32
    flat = embed.reshape(CELLS, WIDTH)
    place = jnp.stack([lax.axis_index("core"), lax.axis_index(TILE)])
    resp_shapes = [((count, CELLS), f32), ((count, WIDTH), f32), ((count, WIDTH), f32)]

    scores, resp, near, far, spread, mask = start(
        place, weights0.reshape(1, count), flat, tissue.reshape(2, WIDTH), means0, whiten0
    )
    shared = swap_all(spread, BRICK)
    for _ in range(SWEEPS):
        resp, near, far = sweep(place, scores, resp, near, far, mask)

    part = swap_all(resp.reshape(8, 8, CELLS), BRICK)
    packets, turned, total = call(
        moments_kernel,
        [((8, PACKET, WIDTH), f32), ((8, WIDTH, CELLS), jnp.bfloat16), ((1, WIDTH), f32)],
        part, shared, flops=1 << 30,
    )
    (packets,) = call(gather_kernel, [((8, PACKET, WIDTH), f32)], swap_all(packets, NEAR))
    packets = swap_all(packets, FAR)
    (packets,) = call(factor_kernel, [((8, PACKET, WIDTH), f32)], packets, flops=1 << 27)
    packets = swap_all(packets, NEAR)
    (part,) = call(
        second_kernel, [((8, 8, CELLS + WIDTH), f32)], packets, turned, flops=1 << 29
    )
    part = swap_all(part, BRICK).reshape(count, CELLS + WIDTH)

    sizes = [lax.axis_size(axes) for axes in ROUND]
    scores, resp, near, far, means_out, totals = call(
        likely_kernel,
        [((count, CELLS), f32)] + resp_shapes + [((2, WIDTH), f32), ((sizes[0], 1, WIDTH), f32)],
        place, part, mask, total, scalars=1,
    )
    totals = jnp.sum(swap_all(totals, ROUND[0]), axis=0)
    totals = swap_all(jnp.broadcast_to(totals[None], (sizes[1], 1, WIDTH)), ROUND[1])
    for _ in range(SWEEPS):
        resp, near, far = sweep(place, scores, resp, near, far, mask)
    totals, resp = lax.optimization_barrier((totals, resp))
    totals = jnp.sum(totals, axis=0)
    bins = CELLS * sizes[0] * sizes[1]
    score = (totals[0, 0] - totals[0, 1] * jnp.log(totals[0, 2])) / bins
    return (resp.reshape(count, 1, 2, WIDTH), means_out, score)


def solution(mesh):
    bits = Mesh(mesh.devices.reshape((2,) * 9), SLAB + TILE)
    in_specs = (P(SLAB, TILE, None, None), P(SLAB, TILE, None), P(), P(), P())
    out_specs = (P(None, SLAB, TILE, None), P(TILE, None), P())
    return jax.shard_map(shards, mesh=bits, in_specs=in_specs, out_specs=out_specs, check_vma=False)
```

```python
import jax
import jax.numpy as jnp
from jax import lax
from jax.experimental import pallas as pl
from jax.experimental.pallas import tpu as pltpu
from jax.sharding import Mesh
from jax.sharding import PartitionSpec as P

SWEEPS = 2
BETA_POTTS = 1.0
COV_RIDGE = 0.01

SLAB = ("x1", "x0", "z2", "z1")
TILE = ("z0", "y2", "y1", "y0", "core")
BRICK = ("x1", "x0", "core")
NEAR = ("y2", "y1", "y0")
FAR = ("z2", "z1", "z0")
ROUND = (("y2", "y1", "y0", "core"), ("x1", "x0", "z2", "z1", "z0"))

WIDTH = 128
CELLS = 256
DEVICES = 512
HALF = 64
PACKET = HALF + 8
VMEM = pl.BlockSpec(memory_space=pltpu.VMEM)
SMEM = pl.BlockSpec(memory_space=pltpu.SMEM)
HBM = pl.BlockSpec(memory_space=pl.ANY)
PARAMS = pltpu.CompilerParams(vmem_limit_bytes=40 * 1024 * 1024)


def call(kernel, shapes, *args, scalars=0, flops=1 << 20):
    out = [jax.ShapeDtypeStruct(shape, kind) for shape, kind in shapes]
    return pl.pallas_call(
        kernel,
        out_shape=out,
        in_specs=[SMEM] * scalars + [VMEM] * (len(args) - scalars),
        out_specs=[VMEM] * len(out),
        compiler_params=PARAMS,
        cost_estimate=pl.CostEstimate(flops=flops, bytes_accessed=1 << 20, transcendentals=0),
    )(*args)


def iotas(shape):
    return (
        lax.broadcasted_iota(jnp.int32, shape, 0),
        lax.broadcasted_iota(jnp.int32, shape, 1),
    )


def matmul(lhs, rhs, dims=((1,), (0,))):
    return lax.dot_general(lhs, rhs, (dims, ((), ())), preferred_element_type=jnp.float32)


def normalise(scores):
    top = jnp.max(scores, axis=0, keepdims=True)
    expon = jnp.exp(scores - top)
    return expon / jnp.sum(expon, axis=0, keepdims=True)


def keep(scores, resp, mask, state):
    count = scores.shape[0]
    state[:count] = scores
    state[count : 2 * count] = resp
    state[2 * count :] = jnp.broadcast_to(mask, (state.shape[0] - 2 * count, CELLS))


def put(core, resp, resp_ref, near_ref, far_ref):
    first, last = resp[:, :WIDTH], resp[:, WIDTH:]
    resp_ref[...] = resp
    near_ref[...] = jnp.where(core == 0, last, first)
    far_ref[...] = jnp.where(core == 0, first, last)


CHUNK = 16


def start_kernel(
    core, weights, flat, tissue, means, whiten,
    state, resp, near, far, spread,
    weights_in, flat_in, tissue_in, means_in, whiten_in, diag, sems,
):
    count = whiten.shape[0]
    small = zip((flat, means, tissue, weights), (flat_in, means_in, tissue_in, weights_in))
    copies = [pltpu.make_async_copy(src, dst, sems.at[n]) for n, (src, dst) in enumerate(small)]
    blocks = [
        pltpu.make_async_copy(
            whiten.at[pl.ds(begin, CHUNK)],
            whiten_in.at[pl.ds(begin, CHUNK)],
            sems.at[4 + begin // CHUNK],
        )
        for begin in range(0, count, CHUNK)
    ]
    for copy in copies + blocks:
        copy.start()
    row_at, col_at = iotas((WIDTH, WIDTH))
    copies[0].wait()
    full = flat_in[...].astype(jnp.float32)
    cells = full.T.astype(jnp.bfloat16)
    for n in range(spread.shape[0]):
        spread[n] = full
    for copy in copies[1:]:
        copy.wait()
    for n, block in enumerate(blocks):
        block.wait()
        for own in range(n * CHUNK, (n + 1) * CHUNK):
            matrix = whiten_in[own]
            full = matrix.astype(jnp.float32)
            shift = jnp.sum(full * means_in[own : own + 1], axis=1, keepdims=True)
            proj = matmul(matrix, cells) - shift
            state[own : own + 1] = jnp.sum(proj * proj, axis=0, keepdims=True)
            diag[own : own + 1] = jnp.sum(
                jnp.where(row_at == col_at, full, 0.0), axis=0, keepdims=True
            )
    prior = weights_in[...]
    prior = jnp.log(prior / jnp.sum(prior, axis=1, keepdims=True))
    row_at, col_at = iotas((count, count))
    prior = jnp.where(row_at == col_at, jnp.broadcast_to(prior, (count, count)), 0.0)
    offset = jnp.sum(prior, axis=1, keepdims=True) + jnp.sum(
        jnp.log(diag[...]), axis=1, keepdims=True
    )
    result = offset - 0.5 * state[:count]
    tissue_f = tissue_in[...].astype(jnp.float32)
    tissue_f = jnp.concatenate([tissue_f[:1], tissue_f[1:]], axis=1)
    first = normalise(result) * tissue_f
    keep(result, first, tissue_f, state)
    put(core[0], first, resp, near, far)


def start(core, weights, flat, tissue, means, whiten):
    count = whiten.shape[0]
    f32 = jnp.float32
    shapes = [(2 * count + 8, CELLS), (count, CELLS), (count, WIDTH), (count, WIDTH)]
    shapes += [(4, CELLS, WIDTH)]
    return pl.pallas_call(
        start_kernel,
        out_shape=[jax.ShapeDtypeStruct(shape, f32) for shape in shapes],
        in_specs=[SMEM] + [HBM] * 5,
        out_specs=[VMEM] * len(shapes),
        scratch_shapes=[
            pltpu.VMEM(weights.shape, f32),
            pltpu.VMEM(flat.shape, flat.dtype),
            pltpu.VMEM(tissue.shape, tissue.dtype),
            pltpu.VMEM(means.shape, f32),
            pltpu.VMEM(whiten.shape, whiten.dtype),
            pltpu.VMEM((count, WIDTH), f32),
            pltpu.SemaphoreType.DMA((4 + count // CHUNK,)),
        ],
        compiler_params=pltpu.CompilerParams(vmem_limit_bytes=58 * 1024 * 1024),
        cost_estimate=pl.CostEstimate(flops=1 << 29, bytes_accessed=1 << 21, transcendentals=0),
    )(core, weights, flat, tissue, means, whiten)


def swept(core, state, resp, slab_even, slab_odd, near_in, far_in):
    count = resp.shape[0]
    lane = iotas((count, WIDTH))[1]
    rows = (resp[:, :WIDTH], resp[:, WIDTH:])
    below = jnp.where(core[0] == 0, far_in[...], near_in[...])
    above = jnp.where(core[0] == 0, near_in[...], far_in[...])
    fields = []
    for row, others in zip(rows, (below + rows[1], rows[0] + above)):
        after = jnp.where(lane < WIDTH - 1, pltpu.roll(row, WIDTH - 1, 1), 0.0)
        before = jnp.where(lane > 0, pltpu.roll(row, 1, 1), 0.0)
        fields.append(others + after + before)
    field = jnp.concatenate(fields, axis=1) + slab_even[...] + slab_odd[...]
    scores, mask = state[:count], state[2 * count : 2 * count + 1]
    return normalise(scores + BETA_POTTS * field) * mask


def first_kernel(core, state, slab_even, slab_odd, near_in, far_in, out, near, far):
    count = out.shape[0]
    resp = state[count : 2 * count]
    put(core[0], swept(core, state, resp, slab_even, slab_odd, near_in, far_in), out, near, far)


def later_kernel(core, state, resp, slab_even, slab_odd, near_in, far_in, out):
    out[...] = swept(core, state, resp[...], slab_even, slab_odd, near_in, far_in)


def last_kernel(core, state, resp, slab_even, slab_odd, near_in, far_in, totals, out, score):
    result = swept(core, state, resp[...], slab_even, slab_odd, near_in, far_in)
    out[:, 0, :] = result[:, :WIDTH]
    out[:, 1, :] = result[:, WIDTH:]
    total = totals[0]
    for n in range(1, totals.shape[0]):
        total = total + totals[n]
    lane = iotas((1, WIDTH))[1]
    lse = jnp.sum(jnp.where(lane == 0, total, 0.0))
    level = jnp.sum(jnp.where(lane == 2, jnp.log(total), 0.0))
    cells = jnp.sum(jnp.where(lane == 1, total, 0.0))
    score[0, 0] = (lse - cells * level) / (CELLS * DEVICES)


def swapped(part, axes, begin):
    count = lax.axis_size(axes)
    pairs = [(i, i + 1) for i in range(begin, count - 1, 2)]
    return lax.ppermute(part, axes, pairs + [(j, i) for i, j in pairs])


def halos(resp, near, far):
    return (
        swapped(resp, SLAB, 0), swapped(resp, SLAB, 1), swapped(near, TILE, 0), swapped(far, TILE, 1)
    )


def moments_kernel(core, resp, mine, theirs, packet, turned, total):
    blocks, count = resp.shape[:2]
    row_at, col_at = iotas((WIDTH, WIDTH))
    ones = jnp.ones((CELLS, WIDTH), jnp.bfloat16)
    acc = [jnp.zeros((WIDTH, 2 * WIDTH), jnp.float32) for _ in range(count)]
    for n in range(blocks):
        cells = mine[n // 2] if n % 2 == 0 else theirs[n // 2]
        block = n + core[0] if n % 2 == 0 else n - core[0]
        weight = resp[block]
        flipped = cells.T
        turned[block] = flipped.astype(jnp.bfloat16)
        wide = jnp.concatenate([cells.astype(jnp.bfloat16), ones], axis=1)
        for k in range(count):
            weighted = (flipped * weight[k : k + 1]).astype(jnp.bfloat16)
            acc[k] = acc[k] + matmul(weighted, wide)
    firsts = jnp.zeros((WIDTH, WIDTH), jnp.float32)
    for k in range(count):
        firsts = jnp.where(col_at == k, acc[k][:, WIDTH:], firsts)
    firsts = firsts.T
    counts = jnp.sum(jnp.sum(resp[...], axis=0), axis=1, keepdims=True)
    counts = jnp.broadcast_to(counts, (count, WIDTH))
    total[...] = jnp.sum(counts, axis=0, keepdims=True)
    fold_row, fold_col = iotas((HALF, WIDTH))
    for k in range(count):
        sym = acc[k][:, :WIDTH]
        sym = sym + sym.T
        low = (fold_col < HALF) | (fold_row > fold_col - HALF)
        packet[k, :HALF] = jnp.where(low, sym[HALF:], pltpu.roll(sym[:HALF], HALF, 1))
        diag = jnp.sum(jnp.where(row_at == col_at, sym, 0.0), axis=0, keepdims=True)
        packet[k, HALF:] = jnp.concatenate(
            [diag, firsts[k : k + 1], counts[k : k + 1], jnp.zeros((5, WIDTH), jnp.float32)],
            axis=0,
        )


def gather_kernel(packets, out):
    total = jnp.sum(packets[...], axis=0)
    for k in range(out.shape[0]):
        out[k] = total


def split(value):
    high = value.astype(jnp.bfloat16).astype(jnp.float32)
    rest = value - high
    middle = rest.astype(jnp.bfloat16).astype(jnp.float32)
    return high, middle, rest - middle


STEP = 16


def whiten_chain(cov):
    row_at, col_at = iotas((WIDTH, WIDTH))
    wide = (STEP, 2 * WIDTH)
    rest = jnp.concatenate([cov, jnp.where(row_at == col_at, 1.0, 0.0)], axis=1)
    sub = lax.broadcasted_iota(jnp.int32, (STEP, WIDTH), 0)
    done, scales = [], []
    for begin in range(0, WIDTH, STEP):
        panel = rest[:STEP]
        cols = [
            jnp.broadcast_to(panel[:, begin + j : begin + j + 1], (STEP, WIDTH))
            for j in range(STEP)
        ]
        scale = jnp.broadcast_to(cols[0][:1], (STEP, WIDTH))
        for j in range(STEP - 1):
            inverse = 1.0 / cols[j][j : j + 1]
            mult = jnp.where(sub > j, cols[j] * inverse, 0.0)
            for l in range(j + 1, STEP):
                cols[l] = cols[l] - mult * jnp.broadcast_to(cols[l][j : j + 1], (STEP, WIDTH))
            both = jnp.concatenate([mult, mult], axis=1)
            panel = panel - both * jnp.broadcast_to(panel[j : j + 1], wide)
            pivot = jnp.broadcast_to(cols[j + 1][j + 1 : j + 2], (STEP, WIDTH))
            scale = jnp.where(sub > j, pivot, scale)
        root = lax.rsqrt(scale)
        panel = panel * jnp.concatenate([root, root], axis=1)
        scales.append(scale)
        done.append(panel[:, WIDTH:])
        if begin + STEP < WIDTH:
            high, middle, low = split(panel)
            right = jnp.concatenate([high, middle, low, high, middle, high], axis=0)
            high, middle, low = (part[:, :WIDTH] for part in (high, middle, low))
            left = jnp.concatenate([high, high, high, middle, middle, low], axis=0)
            update = matmul(left.astype(jnp.bfloat16), right.astype(jnp.bfloat16), ((0,), (0,)))
            rest = rest[STEP:] - update[begin + STEP :]
    logdet = -0.5 * jnp.sum(jnp.log(jnp.concatenate(scales, axis=0)), axis=0, keepdims=True)
    return jnp.concatenate(done, axis=0), logdet


def unfolded(fold):
    both = jnp.concatenate([pltpu.roll(fold, HALF, 1), fold], axis=0)
    return both, both.T


def factor_kernel(packets, out):
    row_at, col_at = iotas((WIDTH, WIDTH))
    packet = jnp.sum(packets[...], axis=0)
    both, turned = unfolded(packet[:HALF])
    diag, first, counts = (packet[HALF + n : HALF + n + 1] for n in range(3))
    left = col_at < HALF
    kept = (left & (row_at <= col_at)) | ((row_at >= HALF) & (left | (row_at > col_at)))
    sym = jnp.where(row_at == col_at, diag, jnp.where(kept, both, turned))
    centre = first / counts
    tall = jnp.broadcast_to(centre, (WIDTH, WIDTH))
    cov = 0.5 * sym / counts - tall.T * tall
    cov = jnp.where(row_at == col_at, cov + COV_RIDGE, cov)
    whiten, logdet = whiten_chain(cov)
    shift = jnp.sum(whiten * tall, axis=1, keepdims=True)
    shift = jnp.broadcast_to(shift, (WIDTH, WIDTH)).T[:1]
    offset = jnp.log(counts) + logdet
    diag = jnp.sum(jnp.where(row_at == col_at, whiten, 0.0), axis=0, keepdims=True)
    fold_row, fold_col = iotas((HALF, WIDTH))
    low = (fold_col < HALF) | (fold_row >= fold_col - HALF)
    fold = jnp.where(low, whiten[HALF:], pltpu.roll(whiten.T[:HALF], HALF, 1))
    zeros = jnp.zeros((4, WIDTH), jnp.float32)
    result = jnp.concatenate([fold, diag, shift, centre, offset, zeros], axis=0)
    for k in range(out.shape[0]):
        out[k] = result


def second_kernel(packets, turned, scores):
    row_at, col_at = iotas((WIDTH, WIDTH))
    top, left = row_at < HALF, col_at < HALF
    below = (row_at >= HALF) & (left | (row_at >= col_at))
    above = top & (row_at > col_at)
    for k in range(packets.shape[0]):
        both, flipped = unfolded(packets[k, :HALF])
        diag, shift, centre, offset = (packets[k, HALF + n : HALF + n + 1] for n in range(4))
        whiten = jnp.where(below, both, jnp.where(above, flipped, 0.0))
        half = jnp.where(top & (row_at == col_at), diag, whiten).astype(jnp.bfloat16)
        shift = jnp.broadcast_to(shift, (WIDTH, WIDTH)).T
        shift = jnp.concatenate([shift, shift], axis=1)
        offset = jnp.concatenate([offset, offset], axis=1)
        for block in range(turned.shape[0]):
            proj = matmul(half, turned[block]) - shift
            quad = jnp.sum(proj * proj, axis=0, keepdims=True)
            scores[block, k : k + 1, :CELLS] = offset - 0.5 * quad
            scores[block, k : k + 1, CELLS:] = centre


def likely_kernel(core, tile, part, mask, total, state, resp, near, far, means, totals):
    values = part[:, :CELLS]
    row = iotas((part.shape[0], WIDTH))[0]
    for n in range(2):
        own = jnp.where(row == 2 * tile[0] + n, part[:, CELLS:], 0.0)
        means[n : n + 1] = jnp.sum(own, axis=0, keepdims=True)
    tissue_f = mask[2 * part.shape[0] : 2 * part.shape[0] + 1]
    top = jnp.max(values, axis=0, keepdims=True)
    expon = jnp.exp(values - top)
    weight = jnp.sum(expon, axis=0, keepdims=True)
    first = expon / weight * tissue_f
    keep(values, first, tissue_f, state)
    put(core[0], first, resp, near, far)
    lse = jnp.sum((top + jnp.log(weight)) * tissue_f, axis=1, keepdims=True)
    cells = jnp.sum(tissue_f, axis=1, keepdims=True)
    lane = iotas((1, WIDTH))[1]
    result = jnp.where(lane == 0, lse, jnp.where(lane == 1, cells, total[...]))
    for n in range(totals.shape[0]):
        totals[n] = result


def swap_all(value, axes):
    return lax.all_to_all(value, axes, 0, 0, tiled=True)


def shards(embed, tissue, whiten0, means0, weights0):
    count = whiten0.shape[0]
    f32 = jnp.float32
    flat = embed.reshape(CELLS, WIDTH)
    core = lax.axis_index("core").reshape(1)
    tile = lax.axis_index(TILE).reshape(1)
    resp_shapes = [((count, CELLS), f32), ((count, WIDTH), f32), ((count, WIDTH), f32)]
    state_shape = ((2 * count + 8, CELLS), f32)

    before, resp, near, far, spread = start(
        core, weights0.reshape(1, count), flat, tissue.reshape(2, WIDTH), means0, whiten0
    )
    mine = swap_all(spread, BRICK[:2])
    resp, near, far = call(
        first_kernel, resp_shapes, core, before, *halos(resp, near, far), scalars=1
    )
    resp, near, far, mine = lax.optimization_barrier((resp, near, far, mine))
    theirs = lax.ppermute(mine, "core", [(0, 1), (1, 0)])
    (resp,) = call(
        later_kernel, resp_shapes[:1], core, before, resp, *halos(resp, near, far), scalars=1
    )
    resp, theirs = lax.optimization_barrier((resp, theirs))

    part = swap_all(resp.reshape(8, 8, CELLS), BRICK)
    packets, turned, total = call(
        moments_kernel,
        [((8, PACKET, WIDTH), f32), ((8, WIDTH, CELLS), jnp.bfloat16), ((1, WIDTH), f32)],
        core, part, mine, theirs, scalars=1, flops=1 << 30,
    )
    (packets,) = call(gather_kernel, [((8, PACKET, WIDTH), f32)], swap_all(packets, NEAR))
    packets = swap_all(packets, FAR)
    (packets,) = call(factor_kernel, [((8, PACKET, WIDTH), f32)], packets, flops=1 << 27)
    packets = swap_all(packets, NEAR)
    (part,) = call(
        second_kernel, [((8, 8, CELLS + WIDTH), f32)], packets, turned, flops=1 << 29
    )
    part = swap_all(part, BRICK).reshape(count, CELLS + WIDTH)

    sizes = [lax.axis_size(axes) for axes in ROUND]
    state, resp, near, far, means_out, totals = call(
        likely_kernel,
        [state_shape] + resp_shapes + [((2, WIDTH), f32), ((sizes[0], 1, WIDTH), f32)],
        core, tile, part, before, total, scalars=2,
    )
    totals = swap_all(totals, ROUND[0])
    resp, near, far = call(
        first_kernel, resp_shapes, core, state, *halos(resp, near, far), scalars=1
    )
    totals, resp, near, far = lax.optimization_barrier((totals, resp, near, far))
    totals = jnp.broadcast_to(jnp.sum(totals, axis=0)[None], (sizes[1], 1, WIDTH))
    totals = swap_all(totals, ROUND[1])
    sides = halos(resp, near, far)
    resp_final, score = pl.pallas_call(
        last_kernel,
        out_shape=[
            jax.ShapeDtypeStruct((count, 2, WIDTH), f32), jax.ShapeDtypeStruct((1, 1), f32)
        ],
        in_specs=[SMEM] + [VMEM] * 7,
        out_specs=[VMEM, SMEM],
        compiler_params=PARAMS,
    )(core, state, resp, *sides, totals)
    return (resp_final.reshape(count, 1, 2, WIDTH), means_out, score.reshape(()))


def solution(mesh):
    bits = Mesh(mesh.devices.reshape((2,) * 9), SLAB + TILE)
    in_specs = (P(SLAB, TILE, None, None), P(SLAB, TILE, None), P(), P(), P())
    out_specs = (P(None, SLAB, TILE, None), P(TILE, None), P())
    return jax.shard_map(shards, mesh=bits, in_specs=in_specs, out_specs=out_specs, check_vma=False)
```

```python
import jax
import jax.numpy as jnp
from jax import lax
from jax.experimental import pallas as pl
from jax.experimental.pallas import tpu as pltpu
from jax.sharding import Mesh
from jax.sharding import PartitionSpec as P

SWEEPS = 2
BETA_POTTS = 1.0
COV_RIDGE = 0.01

SLAB = ("x1", "x0", "z2", "z1")
TILE = ("z0", "y2", "y1", "y0", "core")
BRICK = ("x1", "x0", "core")
NEAR = ("y2", "y1", "y0")
FAR = ("z2", "z1", "z0")
ROUND = (("y2", "y1", "y0", "core"), ("x1", "x0", "z2", "z1", "z0"))

WIDTH = 128
CELLS = 256
DEVICES = 512
HALF = 64
PACKET = HALF + 8
VMEM = pl.BlockSpec(memory_space=pltpu.VMEM)
SMEM = pl.BlockSpec(memory_space=pltpu.SMEM)
HBM = pl.BlockSpec(memory_space=pl.ANY)
PARAMS = pltpu.CompilerParams(vmem_limit_bytes=40 * 1024 * 1024)


def call(kernel, shapes, *args, scalars=0, flops=1 << 20):
    out = [jax.ShapeDtypeStruct(shape, kind) for shape, kind in shapes]
    return pl.pallas_call(
        kernel,
        out_shape=out,
        in_specs=[SMEM] * scalars + [VMEM] * (len(args) - scalars),
        out_specs=[VMEM] * len(out),
        compiler_params=PARAMS,
        cost_estimate=pl.CostEstimate(flops=flops, bytes_accessed=1 << 20, transcendentals=0),
    )(*args)


def iotas(shape):
    return (
        lax.broadcasted_iota(jnp.int32, shape, 0),
        lax.broadcasted_iota(jnp.int32, shape, 1),
    )


def matmul(lhs, rhs, dims=((1,), (0,))):
    return lax.dot_general(lhs, rhs, (dims, ((), ())), preferred_element_type=jnp.float32)


def normalise(scores):
    top = jnp.max(scores, axis=0, keepdims=True)
    expon = jnp.exp(scores - top)
    return expon / jnp.sum(expon, axis=0, keepdims=True)


def keep(scores, resp, mask, state):
    count = scores.shape[0]
    state[:count] = scores
    state[count : 2 * count] = resp
    state[2 * count :] = jnp.broadcast_to(mask, (state.shape[0] - 2 * count, CELLS))


def put(core, resp, resp_ref, near_ref, far_ref):
    first, last = resp[:, :WIDTH], resp[:, WIDTH:]
    resp_ref[...] = resp
    near_ref[...] = jnp.where(core == 0, last, first)
    far_ref[...] = jnp.where(core == 0, first, last)


CHUNK = 16


def start_kernel(
    core, weights, flat, tissue, means, whiten,
    state, resp, near, far, spread,
    weights_in, flat_in, tissue_in, means_in, whiten_in, diag, sems,
):
    count = whiten.shape[0]
    small = zip((flat, means, tissue, weights), (flat_in, means_in, tissue_in, weights_in))
    copies = [pltpu.make_async_copy(src, dst, sems.at[n]) for n, (src, dst) in enumerate(small)]
    blocks = [
        pltpu.make_async_copy(
            whiten.at[pl.ds(begin, CHUNK)],
            whiten_in.at[pl.ds(begin, CHUNK)],
            sems.at[4 + begin // CHUNK],
        )
        for begin in range(0, count, CHUNK)
    ]
    for copy in copies + blocks:
        copy.start()
    row_at, col_at = iotas((WIDTH, WIDTH))
    copies[0].wait()
    full = flat_in[...].astype(jnp.float32)
    cells = full.T.astype(jnp.bfloat16)
    for n in range(spread.shape[0]):
        spread[n] = full
    for copy in copies[1:]:
        copy.wait()
    for n, block in enumerate(blocks):
        block.wait()
        for own in range(n * CHUNK, (n + 1) * CHUNK):
            matrix = whiten_in[own]
            full = matrix.astype(jnp.float32)
            shift = jnp.sum(full * means_in[own : own + 1], axis=1, keepdims=True)
            proj = matmul(matrix, cells) - shift
            state[own : own + 1] = jnp.sum(proj * proj, axis=0, keepdims=True)
            diag[own : own + 1] = jnp.sum(
                jnp.where(row_at == col_at, full, 0.0), axis=0, keepdims=True
            )
    prior = weights_in[...]
    prior = jnp.log(prior / jnp.sum(prior, axis=1, keepdims=True))
    row_at, col_at = iotas((count, count))
    prior = jnp.where(row_at == col_at, jnp.broadcast_to(prior, (count, count)), 0.0)
    offset = jnp.sum(prior, axis=1, keepdims=True) + jnp.sum(
        jnp.log(diag[...]), axis=1, keepdims=True
    )
    result = offset - 0.5 * state[:count]
    tissue_f = tissue_in[...].astype(jnp.float32)
    tissue_f = jnp.concatenate([tissue_f[:1], tissue_f[1:]], axis=1)
    first = normalise(result) * tissue_f
    keep(result, first, tissue_f, state)
    put(core[0], first, resp, near, far)


def start(core, weights, flat, tissue, means, whiten):
    count = whiten.shape[0]
    f32 = jnp.float32
    shapes = [(2 * count + 8, CELLS), (count, CELLS), (count, WIDTH), (count, WIDTH)]
    shapes += [(4, CELLS, WIDTH)]
    return pl.pallas_call(
        start_kernel,
        out_shape=[jax.ShapeDtypeStruct(shape, f32) for shape in shapes],
        in_specs=[SMEM] + [HBM] * 5,
        out_specs=[VMEM] * len(shapes),
        scratch_shapes=[
            pltpu.VMEM(weights.shape, f32),
            pltpu.VMEM(flat.shape, flat.dtype),
            pltpu.VMEM(tissue.shape, tissue.dtype),
            pltpu.VMEM(means.shape, f32),
            pltpu.VMEM(whiten.shape, whiten.dtype),
            pltpu.VMEM((count, WIDTH), f32),
            pltpu.SemaphoreType.DMA((4 + count // CHUNK,)),
        ],
        compiler_params=pltpu.CompilerParams(vmem_limit_bytes=58 * 1024 * 1024),
        cost_estimate=pl.CostEstimate(flops=1 << 29, bytes_accessed=1 << 21, transcendentals=0),
    )(core, weights, flat, tissue, means, whiten)


def swept(core, state, resp, slab_even, slab_odd, near_in, far_in):
    count = resp.shape[0]
    lane = iotas((count, WIDTH))[1]
    rows = (resp[:, :WIDTH], resp[:, WIDTH:])
    below = jnp.where(core[0] == 0, far_in[...], near_in[...])
    above = jnp.where(core[0] == 0, near_in[...], far_in[...])
    fields = []
    for row, others in zip(rows, (below + rows[1], rows[0] + above)):
        after = jnp.where(lane < WIDTH - 1, pltpu.roll(row, WIDTH - 1, 1), 0.0)
        before = jnp.where(lane > 0, pltpu.roll(row, 1, 1), 0.0)
        fields.append(others + after + before)
    field = jnp.concatenate(fields, axis=1) + slab_even[...] + slab_odd[...]
    scores, mask = state[:count], state[state.shape[0] - 1 :]
    return normalise(scores + BETA_POTTS * field) * mask


def first_kernel(core, state, slab_even, slab_odd, near_in, far_in, out, near, far):
    count = out.shape[0]
    resp = state[count : 2 * count]
    put(core[0], swept(core, state, resp, slab_even, slab_odd, near_in, far_in), out, near, far)


def early_kernel(core, state, slab_even, slab_odd, near_in, far_in, out, near, far, kept):
    count = out.shape[0]
    kept[:count] = state[:count]
    kept[count:] = state[2 * count :]
    first_kernel(core, state, slab_even, slab_odd, near_in, far_in, out, near, far)


def later_kernel(core, state, resp, slab_even, slab_odd, near_in, far_in, out):
    out[...] = swept(core, state, resp[...], slab_even, slab_odd, near_in, far_in)


def last_kernel(core, state, resp, slab_even, slab_odd, near_in, far_in, totals, out, score):
    result = swept(core, state, resp[...], slab_even, slab_odd, near_in, far_in)
    out[:, 0, :] = result[:, :WIDTH]
    out[:, 1, :] = result[:, WIDTH:]
    total = totals[0]
    for n in range(1, totals.shape[0]):
        total = total + totals[n]
    total = total[:1]
    lane = iotas((1, WIDTH))[1]
    lse = jnp.sum(jnp.where(lane == 0, total, 0.0))
    level = jnp.sum(jnp.where(lane == 2, jnp.log(total), 0.0))
    cells = jnp.sum(jnp.where(lane == 1, total, 0.0))
    score[0, 0] = (lse - cells * level) / (CELLS * DEVICES)


def swapped(part, axes, begin):
    count = lax.axis_size(axes)
    pairs = [(i, i + 1) for i in range(begin, count - 1, 2)]
    return lax.ppermute(part, axes, pairs + [(j, i) for i, j in pairs])


def halos(resp, near, far):
    return (
        swapped(resp, SLAB, 0), swapped(resp, SLAB, 1), swapped(near, TILE, 0), swapped(far, TILE, 1)
    )


def moments_kernel(core, resp, mine, theirs, packet, turned, total):
    blocks, count = resp.shape[:2]
    row_at, col_at = iotas((WIDTH, WIDTH))
    ones = jnp.ones((CELLS, WIDTH), jnp.bfloat16)
    acc = [jnp.zeros((WIDTH, 2 * WIDTH), jnp.float32) for _ in range(count)]
    for n in range(blocks):
        cells = mine[n // 2] if n % 2 == 0 else theirs[n // 2]
        block = n + core[0] if n % 2 == 0 else n - core[0]
        weight = resp[block]
        flipped = cells.T
        turned[block] = flipped.astype(jnp.bfloat16)
        wide = jnp.concatenate([cells.astype(jnp.bfloat16), ones], axis=1)
        for k in range(count):
            weighted = (flipped * weight[k : k + 1]).astype(jnp.bfloat16)
            acc[k] = acc[k] + matmul(weighted, wide)
    firsts = jnp.zeros((WIDTH, WIDTH), jnp.float32)
    for k in range(count):
        firsts = jnp.where(col_at == k, acc[k][:, WIDTH:], firsts)
    firsts = firsts.T
    counts = jnp.sum(jnp.sum(resp[...], axis=0), axis=1, keepdims=True)
    counts = jnp.broadcast_to(counts, (count, WIDTH))
    total[...] = jnp.sum(counts, axis=0, keepdims=True)
    fold_row, fold_col = iotas((HALF, WIDTH))
    for k in range(count):
        sym = acc[k][:, :WIDTH]
        sym = sym + sym.T
        low = (fold_col < HALF) | (fold_row > fold_col - HALF)
        packet[k, :HALF] = jnp.where(low, sym[HALF:], pltpu.roll(sym[:HALF], HALF, 1))
        diag = jnp.sum(jnp.where(row_at == col_at, sym, 0.0), axis=0, keepdims=True)
        packet[k, HALF:] = jnp.concatenate(
            [diag, firsts[k : k + 1], counts[k : k + 1], jnp.zeros((5, WIDTH), jnp.float32)],
            axis=0,
        )


def gather_kernel(packets, out):
    total = jnp.sum(packets[...], axis=0)
    for k in range(out.shape[0]):
        out[k] = total


def split(value):
    high = value.astype(jnp.bfloat16).astype(jnp.float32)
    rest = value - high
    middle = rest.astype(jnp.bfloat16).astype(jnp.float32)
    return high, middle, rest - middle


STEP = 16


def whiten_chain(cov):
    row_at, col_at = iotas((WIDTH, WIDTH))
    wide = (STEP, 2 * WIDTH)
    rest = jnp.concatenate([cov, jnp.where(row_at == col_at, 1.0, 0.0)], axis=1)
    sub = lax.broadcasted_iota(jnp.int32, (STEP, WIDTH), 0)
    done, scales = [], []
    for begin in range(0, WIDTH, STEP):
        panel = rest[:STEP]
        cols = [
            jnp.broadcast_to(panel[:, begin + j : begin + j + 1], (STEP, WIDTH))
            for j in range(STEP)
        ]
        scale = jnp.broadcast_to(cols[0][:1], (STEP, WIDTH))
        for j in range(STEP - 1):
            inverse = 1.0 / cols[j][j : j + 1]
            mult = jnp.where(sub > j, cols[j] * inverse, 0.0)
            for l in range(j + 1, STEP):
                cols[l] = cols[l] - mult * jnp.broadcast_to(cols[l][j : j + 1], (STEP, WIDTH))
            both = jnp.concatenate([mult, mult], axis=1)
            panel = panel - both * jnp.broadcast_to(panel[j : j + 1], wide)
            pivot = jnp.broadcast_to(cols[j + 1][j + 1 : j + 2], (STEP, WIDTH))
            scale = jnp.where(sub > j, pivot, scale)
        root = lax.rsqrt(scale)
        panel = panel * jnp.concatenate([root, root], axis=1)
        scales.append(scale)
        done.append(panel[:, WIDTH:])
        if begin + STEP < WIDTH:
            high, middle, low = split(panel)
            right = jnp.concatenate([high, middle, low, high, middle, high], axis=0)
            high, middle, low = (part[:, :WIDTH] for part in (high, middle, low))
            left = jnp.concatenate([high, high, high, middle, middle, low], axis=0)
            update = matmul(left.astype(jnp.bfloat16), right.astype(jnp.bfloat16), ((0,), (0,)))
            rest = rest[STEP:] - update[begin + STEP :]
    logdet = -0.5 * jnp.sum(jnp.log(jnp.concatenate(scales, axis=0)), axis=0, keepdims=True)
    return jnp.concatenate(done, axis=0), logdet


def unfolded(fold):
    both = jnp.concatenate([pltpu.roll(fold, HALF, 1), fold], axis=0)
    return both, both.T


def factor_kernel(packets, out):
    row_at, col_at = iotas((WIDTH, WIDTH))
    packet = jnp.sum(packets[...], axis=0)
    both, turned = unfolded(packet[:HALF])
    diag, first, counts = (packet[HALF + n : HALF + n + 1] for n in range(3))
    left = col_at < HALF
    kept = (left & (row_at <= col_at)) | ((row_at >= HALF) & (left | (row_at > col_at)))
    sym = jnp.where(row_at == col_at, diag, jnp.where(kept, both, turned))
    centre = first / counts
    tall = jnp.broadcast_to(centre, (WIDTH, WIDTH))
    cov = 0.5 * sym / counts - tall.T * tall
    cov = jnp.where(row_at == col_at, cov + COV_RIDGE, cov)
    whiten, logdet = whiten_chain(cov)
    shift = jnp.sum(whiten * tall, axis=1, keepdims=True)
    shift = jnp.broadcast_to(shift, (WIDTH, WIDTH)).T[:1]
    offset = jnp.log(counts) + logdet
    diag = jnp.sum(jnp.where(row_at == col_at, whiten, 0.0), axis=0, keepdims=True)
    fold_row, fold_col = iotas((HALF, WIDTH))
    low = (fold_col < HALF) | (fold_row >= fold_col - HALF)
    fold = jnp.where(low, whiten[HALF:], pltpu.roll(whiten.T[:HALF], HALF, 1))
    zeros = jnp.zeros((4, WIDTH), jnp.float32)
    result = jnp.concatenate([fold, diag, shift, centre, offset, zeros], axis=0)
    for k in range(out.shape[0]):
        out[k] = result


def second_kernel(packets, turned, scores):
    row_at, col_at = iotas((WIDTH, WIDTH))
    top, left = row_at < HALF, col_at < HALF
    below = (row_at >= HALF) & (left | (row_at >= col_at))
    above = top & (row_at > col_at)
    count = packets.shape[0]
    halves, shifts, offsets, centres = [], [], [], []
    for k in range(count):
        both, flipped = unfolded(packets[k, :HALF])
        diag, shift, centre, offset = (packets[k, HALF + n : HALF + n + 1] for n in range(4))
        whiten = jnp.where(below, both, jnp.where(above, flipped, 0.0))
        whiten = jnp.where(top & (row_at == col_at), diag, whiten)
        halves.append(whiten.astype(jnp.bfloat16))
        shifts.append(jnp.broadcast_to(shift, (WIDTH, WIDTH)).T)
        offsets.append(offset)
        centres.append(centre)
    halves = jnp.concatenate(halves, axis=0)
    offsets = jnp.concatenate(offsets, axis=0)
    offsets = jnp.concatenate([offsets, offsets], axis=1)
    centres = jnp.concatenate(centres, axis=0)
    for block in range(turned.shape[0]):
        proj = matmul(halves, turned[block])
        quads = []
        for k in range(count):
            shift = jnp.concatenate([shifts[k], shifts[k]], axis=1)
            off = proj[k * WIDTH : (k + 1) * WIDTH] - shift
            quads.append(jnp.sum(off * off, axis=0, keepdims=True))
        scores[block, :, :CELLS] = offsets - 0.5 * jnp.concatenate(quads, axis=0)
        scores[block, :, CELLS:] = centres


def likely_kernel(core, tile, part, mask, total, state, resp, near, far, means, totals):
    values = part[:, :CELLS]
    row = iotas((part.shape[0], WIDTH))[0]
    for n in range(2):
        own = jnp.where(row == 2 * tile[0] + n, part[:, CELLS:], 0.0)
        means[n : n + 1] = jnp.sum(own, axis=0, keepdims=True)
    tissue_f = mask[mask.shape[0] - 1 :]
    top = jnp.max(values, axis=0, keepdims=True)
    expon = jnp.exp(values - top)
    weight = jnp.sum(expon, axis=0, keepdims=True)
    first = expon / weight * tissue_f
    keep(values, first, tissue_f, state)
    put(core[0], first, resp, near, far)
    lse = jnp.sum((top + jnp.log(weight)) * tissue_f, axis=1, keepdims=True)
    cells = jnp.sum(tissue_f, axis=1, keepdims=True)
    lane = iotas((1, WIDTH))[1]
    result = jnp.where(lane == 0, lse, jnp.where(lane == 1, cells, total[...]))
    for n in range(totals.shape[0]):
        totals[n] = jnp.broadcast_to(result, totals.shape[1:])


def swap_all(value, axes):
    return lax.all_to_all(value, axes, 0, 0, tiled=True)


def shards(embed, tissue, whiten0, means0, weights0):
    count = whiten0.shape[0]
    f32 = jnp.float32
    flat = embed.reshape(CELLS, WIDTH)
    core = lax.axis_index("core").reshape(1)
    tile = lax.axis_index(TILE).reshape(1)
    resp_shapes = [((count, CELLS), f32), ((count, WIDTH), f32), ((count, WIDTH), f32)]
    state_shape = ((2 * count + 8, CELLS), f32)

    before, resp, near, far, spread = start(
        core, weights0.reshape(1, count), flat, tissue.reshape(2, WIDTH), means0, whiten0
    )
    mine = swap_all(spread, BRICK[:2])
    kept_shape = ((count + 8, CELLS), f32)
    resp, near, far, kept = call(
        early_kernel, resp_shapes + [kept_shape], core, before, *halos(resp, near, far), scalars=1
    )
    resp, near, far, mine = lax.optimization_barrier((resp, near, far, mine))
    theirs = lax.ppermute(mine, "core", [(0, 1), (1, 0)])
    (resp,) = call(
        later_kernel, resp_shapes[:1], core, kept, resp, *halos(resp, near, far), scalars=1
    )
    resp, theirs = lax.optimization_barrier((resp, theirs))

    part = swap_all(resp.reshape(8, 8, CELLS), BRICK)
    packets, turned, total = call(
        moments_kernel,
        [((8, PACKET, WIDTH), f32), ((8, WIDTH, CELLS), jnp.bfloat16), ((1, WIDTH), f32)],
        core, part, mine, theirs, scalars=1, flops=1 << 30,
    )
    (packets,) = call(gather_kernel, [((8, PACKET, WIDTH), f32)], swap_all(packets, NEAR))
    packets = swap_all(packets, FAR)
    (packets,) = call(factor_kernel, [((8, PACKET, WIDTH), f32)], packets, flops=1 << 27)
    packets = swap_all(packets, NEAR)
    (part,) = call(
        second_kernel, [((8, 8, CELLS + WIDTH), f32)], packets, turned, flops=1 << 29
    )
    part = swap_all(part, BRICK).reshape(count, CELLS + WIDTH)

    sizes = [lax.axis_size(axes) for axes in ROUND]
    state, resp, near, far, means_out, totals = call(
        likely_kernel,
        [state_shape] + resp_shapes + [((2, WIDTH), f32), ((sizes[0], 16, WIDTH), f32)],
        core, tile, part, kept, total, scalars=2,
    )
    totals = swap_all(totals, ROUND[0])
    resp, near, far = call(
        first_kernel, resp_shapes, core, state, *halos(resp, near, far), scalars=1
    )
    totals, resp, near, far = lax.optimization_barrier((totals, resp, near, far))
    totals = jnp.broadcast_to(jnp.sum(totals, axis=0)[None, :8], (sizes[1], 8, WIDTH))
    totals = swap_all(totals, ROUND[1])
    sides = halos(resp, near, far)
    resp_final, score = pl.pallas_call(
        last_kernel,
        out_shape=[
            jax.ShapeDtypeStruct((count, 2, WIDTH), f32), jax.ShapeDtypeStruct((1, 1), f32)
        ],
        in_specs=[SMEM] + [VMEM] * 7,
        out_specs=[VMEM, SMEM],
        compiler_params=PARAMS,
    )(core, state, resp, *sides, totals)
    return (resp_final.reshape(count, 1, 2, WIDTH), means_out, score.reshape(()))


def solution(mesh):
    bits = Mesh(mesh.devices.reshape((2,) * 9), SLAB + TILE)
    in_specs = (P(SLAB, TILE, None, None), P(SLAB, TILE, None), P(), P(), P())
    out_specs = (P(None, SLAB, TILE, None), P(TILE, None), P())
    return jax.shard_map(shards, mesh=bits, in_specs=in_specs, out_specs=out_specs, check_vma=False)
```

```python
import jax
import jax.numpy as jnp
from jax import lax
from jax.experimental import pallas as pl
from jax.experimental.pallas import tpu as pltpu
from jax.sharding import Mesh
from jax.sharding import PartitionSpec as P

SWEEPS = 2
BETA_POTTS = 1.0
COV_RIDGE = 0.01

SLAB = ("x1", "x0", "z2", "z1")
TILE = ("z0", "y2", "y1", "y0", "core")
BRICK = ("x1", "x0", "core")
PLANE = ("z2", "z1", "z0", "y2", "y1", "y0", "core")
ALONG_Y = [[[z * 16 + y * 2 + core for y in range(8)] for z in range(8)] for core in range(2)]
ALONG_Z = [[[z * 16 + y * 2 + core for z in range(8)] for y in range(8)] for core in range(2)]
NEAR = ALONG_Y[0] + ALONG_Z[1]
FAR = ALONG_Z[0] + ALONG_Y[1]
ROUND = (("y2", "y1", "y0", "core"), ("x1", "x0", "z2", "z1", "z0"))

WIDTH = 128
CELLS = 256
DEVICES = 512
HALF = 64
PACKET = HALF + 8
VMEM = pl.BlockSpec(memory_space=pltpu.VMEM)
SMEM = pl.BlockSpec(memory_space=pltpu.SMEM)
HBM = pl.BlockSpec(memory_space=pl.ANY)
PARAMS = pltpu.CompilerParams(vmem_limit_bytes=40 * 1024 * 1024)


def call(kernel, shapes, *args, scalars=0, flops=1 << 20):
    out = [jax.ShapeDtypeStruct(shape, kind) for shape, kind in shapes]
    return pl.pallas_call(
        kernel,
        out_shape=out,
        in_specs=[SMEM] * scalars + [VMEM] * (len(args) - scalars),
        out_specs=[VMEM] * len(out),
        compiler_params=PARAMS,
        cost_estimate=pl.CostEstimate(flops=flops, bytes_accessed=1 << 20, transcendentals=0),
    )(*args)


def iotas(shape):
    return (
        lax.broadcasted_iota(jnp.int32, shape, 0),
        lax.broadcasted_iota(jnp.int32, shape, 1),
    )


def matmul(lhs, rhs, dims=((1,), (0,))):
    return lax.dot_general(lhs, rhs, (dims, ((), ())), preferred_element_type=jnp.float32)


def normalise(scores):
    top = jnp.max(scores, axis=0, keepdims=True)
    expon = jnp.exp(scores - top)
    return expon / jnp.sum(expon, axis=0, keepdims=True)


def keep(scores, resp, mask, state):
    count = scores.shape[0]
    state[:count] = scores
    state[count : 2 * count] = resp
    state[2 * count :] = jnp.broadcast_to(mask, (state.shape[0] - 2 * count, CELLS))


def put(core, resp, resp_ref, near_ref, far_ref):
    first, last = resp[:, :WIDTH], resp[:, WIDTH:]
    resp_ref[...] = resp
    near_ref[...] = jnp.where(core == 0, last, first)
    far_ref[...] = jnp.where(core == 0, first, last)


CHUNK = 16


def start_kernel(
    core, weights, flat, tissue, means, whiten,
    state, resp, near, far, spread,
    weights_in, flat_in, tissue_in, means_in, whiten_in, diag, sems,
):
    count = whiten.shape[0]
    small = zip((flat, means, tissue, weights), (flat_in, means_in, tissue_in, weights_in))
    copies = [pltpu.make_async_copy(src, dst, sems.at[n]) for n, (src, dst) in enumerate(small)]
    blocks = [
        pltpu.make_async_copy(
            whiten.at[pl.ds(begin, CHUNK)],
            whiten_in.at[pl.ds(begin, CHUNK)],
            sems.at[4 + begin // CHUNK],
        )
        for begin in range(0, count, CHUNK)
    ]
    for copy in copies + blocks:
        copy.start()
    row_at, col_at = iotas((WIDTH, WIDTH))
    copies[0].wait()
    full = flat_in[...].astype(jnp.float32)
    cells = full.T.astype(jnp.bfloat16)
    for n in range(spread.shape[0]):
        spread[n] = full
    for copy in copies[1:]:
        copy.wait()
    for n, block in enumerate(blocks):
        block.wait()
        for own in range(n * CHUNK, (n + 1) * CHUNK):
            matrix = whiten_in[own]
            full = matrix.astype(jnp.float32)
            shift = jnp.sum(full * means_in[own : own + 1], axis=1, keepdims=True)
            proj = matmul(matrix, cells) - shift
            state[own : own + 1] = jnp.sum(proj * proj, axis=0, keepdims=True)
            diag[own : own + 1] = jnp.sum(
                jnp.where(row_at == col_at, full, 0.0), axis=0, keepdims=True
            )
    prior = weights_in[...]
    prior = jnp.log(prior / jnp.sum(prior, axis=1, keepdims=True))
    row_at, col_at = iotas((count, count))
    prior = jnp.where(row_at == col_at, jnp.broadcast_to(prior, (count, count)), 0.0)
    offset = jnp.sum(prior, axis=1, keepdims=True) + jnp.sum(
        jnp.log(diag[...]), axis=1, keepdims=True
    )
    result = offset - 0.5 * state[:count]
    tissue_f = tissue_in[...].astype(jnp.float32)
    tissue_f = jnp.concatenate([tissue_f[:1], tissue_f[1:]], axis=1)
    first = normalise(result) * tissue_f
    keep(result, first, tissue_f, state)
    put(core[0], first, resp, near, far)


def start(core, weights, flat, tissue, means, whiten):
    count = whiten.shape[0]
    f32 = jnp.float32
    shapes = [(2 * count + 8, CELLS), (count, CELLS), (count, WIDTH), (count, WIDTH)]
    shapes += [(4, CELLS, WIDTH)]
    return pl.pallas_call(
        start_kernel,
        out_shape=[jax.ShapeDtypeStruct(shape, f32) for shape in shapes],
        in_specs=[SMEM] + [HBM] * 5,
        out_specs=[VMEM] * len(shapes),
        scratch_shapes=[
            pltpu.VMEM(weights.shape, f32),
            pltpu.VMEM(flat.shape, flat.dtype),
            pltpu.VMEM(tissue.shape, tissue.dtype),
            pltpu.VMEM(means.shape, f32),
            pltpu.VMEM(whiten.shape, whiten.dtype),
            pltpu.VMEM((count, WIDTH), f32),
            pltpu.SemaphoreType.DMA((4 + count // CHUNK,)),
        ],
        compiler_params=pltpu.CompilerParams(vmem_limit_bytes=58 * 1024 * 1024),
        cost_estimate=pl.CostEstimate(flops=1 << 29, bytes_accessed=1 << 21, transcendentals=0),
    )(core, weights, flat, tissue, means, whiten)


def swept(core, state, resp, slab_even, slab_odd, near_in, far_in):
    count = resp.shape[0]
    lane = iotas((count, WIDTH))[1]
    rows = (resp[:, :WIDTH], resp[:, WIDTH:])
    below = jnp.where(core[0] == 0, far_in[...], near_in[...])
    above = jnp.where(core[0] == 0, near_in[...], far_in[...])
    fields = []
    for row, others in zip(rows, (below + rows[1], rows[0] + above)):
        after = jnp.where(lane < WIDTH - 1, pltpu.roll(row, WIDTH - 1, 1), 0.0)
        before = jnp.where(lane > 0, pltpu.roll(row, 1, 1), 0.0)
        fields.append(others + after + before)
    field = jnp.concatenate(fields, axis=1) + slab_even[...] + slab_odd[...]
    scores, mask = state[:count], state[state.shape[0] - 1 :]
    return normalise(scores + BETA_POTTS * field) * mask


def first_kernel(core, state, slab_even, slab_odd, near_in, far_in, out, near, far):
    count = out.shape[0]
    resp = state[count : 2 * count]
    put(core[0], swept(core, state, resp, slab_even, slab_odd, near_in, far_in), out, near, far)


def early_kernel(core, state, slab_even, slab_odd, near_in, far_in, out, near, far, kept):
    count = out.shape[0]
    kept[:count] = state[:count]
    kept[count:] = state[2 * count :]
    first_kernel(core, state, slab_even, slab_odd, near_in, far_in, out, near, far)


def later_kernel(core, state, resp, slab_even, slab_odd, near_in, far_in, out):
    out[...] = swept(core, state, resp[...], slab_even, slab_odd, near_in, far_in)


def last_kernel(core, state, resp, slab_even, slab_odd, near_in, far_in, totals, out, score):
    result = swept(core, state, resp[...], slab_even, slab_odd, near_in, far_in)
    out[:, 0, :] = result[:, :WIDTH]
    out[:, 1, :] = result[:, WIDTH:]
    total = totals[0]
    for n in range(1, totals.shape[0]):
        total = total + totals[n]
    total = total[:1]
    lane = iotas((1, WIDTH))[1]
    lse = jnp.sum(jnp.where(lane == 0, total, 0.0))
    level = jnp.sum(jnp.where(lane == 2, jnp.log(total), 0.0))
    cells = jnp.sum(jnp.where(lane == 1, total, 0.0))
    score[0, 0] = (lse - cells * level) / (CELLS * DEVICES)


def swapped(part, axes, begin):
    count = lax.axis_size(axes)
    pairs = [(i, i + 1) for i in range(begin, count - 1, 2)]
    return lax.ppermute(part, axes, pairs + [(j, i) for i, j in pairs])


def halos(resp, near, far):
    return (
        swapped(resp, SLAB, 0), swapped(resp, SLAB, 1), swapped(near, TILE, 0), swapped(far, TILE, 1)
    )


def moments_kernel(core, resp, mine, theirs, packet, turned, total):
    blocks, count = resp.shape[:2]
    row_at, col_at = iotas((WIDTH, WIDTH))
    ones = jnp.ones((CELLS, WIDTH), jnp.bfloat16)
    acc = [jnp.zeros((WIDTH, 2 * WIDTH), jnp.float32) for _ in range(count)]
    for n in range(blocks):
        cells = mine[n // 2] if n % 2 == 0 else theirs[n // 2]
        block = n + core[0] if n % 2 == 0 else n - core[0]
        weight = resp[block]
        flipped = cells.T
        turned[block] = flipped.astype(jnp.bfloat16)
        wide = jnp.concatenate([cells.astype(jnp.bfloat16), ones], axis=1)
        for k in range(count):
            weighted = (flipped * weight[k : k + 1]).astype(jnp.bfloat16)
            acc[k] = acc[k] + matmul(weighted, wide)
    firsts = jnp.zeros((WIDTH, WIDTH), jnp.float32)
    for k in range(count):
        firsts = jnp.where(col_at == k, acc[k][:, WIDTH:], firsts)
    firsts = firsts.T
    counts = jnp.sum(jnp.sum(resp[...], axis=0), axis=1, keepdims=True)
    counts = jnp.broadcast_to(counts, (count, WIDTH))
    total[...] = jnp.sum(counts, axis=0, keepdims=True)
    fold_row, fold_col = iotas((HALF, WIDTH))
    for k in range(count):
        sym = acc[k][:, :WIDTH]
        sym = sym + sym.T
        low = (fold_col < HALF) | (fold_row > fold_col - HALF)
        packet[k, :HALF] = jnp.where(low, sym[HALF:], pltpu.roll(sym[:HALF], HALF, 1))
        diag = jnp.sum(jnp.where(row_at == col_at, sym, 0.0), axis=0, keepdims=True)
        packet[k, HALF:] = jnp.concatenate(
            [diag, firsts[k : k + 1], counts[k : k + 1], jnp.zeros((5, WIDTH), jnp.float32)],
            axis=0,
        )


def gather_kernel(packets, out):
    total = jnp.sum(packets[...], axis=0)
    for k in range(out.shape[0]):
        out[k] = total


def split(value):
    high = value.astype(jnp.bfloat16).astype(jnp.float32)
    rest = value - high
    middle = rest.astype(jnp.bfloat16).astype(jnp.float32)
    return high, middle, rest - middle


STEP = 16


def whiten_chain(cov):
    row_at, col_at = iotas((WIDTH, WIDTH))
    wide = (STEP, 2 * WIDTH)
    rest = jnp.concatenate([cov, jnp.where(row_at == col_at, 1.0, 0.0)], axis=1)
    sub = lax.broadcasted_iota(jnp.int32, (STEP, WIDTH), 0)
    done, scales = [], []
    for begin in range(0, WIDTH, STEP):
        panel = rest[:STEP]
        cols = [
            jnp.broadcast_to(panel[:, begin + j : begin + j + 1], (STEP, WIDTH))
            for j in range(STEP)
        ]
        scale = jnp.broadcast_to(cols[0][:1], (STEP, WIDTH))
        for j in range(STEP - 1):
            inverse = 1.0 / cols[j][j : j + 1]
            mult = jnp.where(sub > j, cols[j] * inverse, 0.0)
            for l in range(j + 1, STEP):
                cols[l] = cols[l] - mult * jnp.broadcast_to(cols[l][j : j + 1], (STEP, WIDTH))
            both = jnp.concatenate([mult, mult], axis=1)
            panel = panel - both * jnp.broadcast_to(panel[j : j + 1], wide)
            pivot = jnp.broadcast_to(cols[j + 1][j + 1 : j + 2], (STEP, WIDTH))
            scale = jnp.where(sub > j, pivot, scale)
        root = lax.rsqrt(scale)
        panel = panel * jnp.concatenate([root, root], axis=1)
        scales.append(scale)
        done.append(panel[:, WIDTH:])
        if begin + STEP < WIDTH:
            high, middle, low = split(panel)
            right = jnp.concatenate([high, middle, low, high, middle, high], axis=0)
            high, middle, low = (part[:, :WIDTH] for part in (high, middle, low))
            left = jnp.concatenate([high, high, high, middle, middle, low], axis=0)
            update = matmul(left.astype(jnp.bfloat16), right.astype(jnp.bfloat16), ((0,), (0,)))
            rest = rest[STEP:] - update[begin + STEP :]
    logdet = -0.5 * jnp.sum(jnp.log(jnp.concatenate(scales, axis=0)), axis=0, keepdims=True)
    return jnp.concatenate(done, axis=0), logdet


def unfolded(fold):
    both = jnp.concatenate([pltpu.roll(fold, HALF, 1), fold], axis=0)
    return both, both.T


def factor_kernel(packets, out):
    row_at, col_at = iotas((WIDTH, WIDTH))
    packet = jnp.sum(packets[...], axis=0)
    both, turned = unfolded(packet[:HALF])
    diag, first, counts = (packet[HALF + n : HALF + n + 1] for n in range(3))
    left = col_at < HALF
    kept = (left & (row_at <= col_at)) | ((row_at >= HALF) & (left | (row_at > col_at)))
    sym = jnp.where(row_at == col_at, diag, jnp.where(kept, both, turned))
    centre = first / counts
    tall = jnp.broadcast_to(centre, (WIDTH, WIDTH))
    cov = 0.5 * sym / counts - tall.T * tall
    cov = jnp.where(row_at == col_at, cov + COV_RIDGE, cov)
    whiten, logdet = whiten_chain(cov)
    shift = jnp.sum(whiten * tall, axis=1, keepdims=True)
    shift = jnp.broadcast_to(shift, (WIDTH, WIDTH)).T[:1]
    offset = jnp.log(counts) + logdet
    diag = jnp.sum(jnp.where(row_at == col_at, whiten, 0.0), axis=0, keepdims=True)
    fold_row, fold_col = iotas((HALF, WIDTH))
    low = (fold_col < HALF) | (fold_row >= fold_col - HALF)
    fold = jnp.where(low, whiten[HALF:], pltpu.roll(whiten.T[:HALF], HALF, 1))
    zeros = jnp.zeros((4, WIDTH), jnp.float32)
    result = jnp.concatenate([fold, diag, shift, centre, offset, zeros], axis=0)
    for k in range(out.shape[0]):
        out[k] = result


def second_kernel(packets, turned, scores):
    row_at, col_at = iotas((WIDTH, WIDTH))
    top, left = row_at < HALF, col_at < HALF
    below = (row_at >= HALF) & (left | (row_at >= col_at))
    above = top & (row_at > col_at)
    count = packets.shape[0]
    halves, shifts, offsets, centres = [], [], [], []
    for k in range(count):
        both, flipped = unfolded(packets[k, :HALF])
        diag, shift, centre, offset = (packets[k, HALF + n : HALF + n + 1] for n in range(4))
        whiten = jnp.where(below, both, jnp.where(above, flipped, 0.0))
        whiten = jnp.where(top & (row_at == col_at), diag, whiten)
        halves.append(whiten.astype(jnp.bfloat16))
        shifts.append(jnp.broadcast_to(shift, (WIDTH, WIDTH)).T)
        offsets.append(offset)
        centres.append(centre)
    halves = jnp.concatenate(halves, axis=0)
    offsets = jnp.concatenate(offsets, axis=0)
    offsets = jnp.concatenate([offsets, offsets], axis=1)
    centres = jnp.concatenate(centres, axis=0)
    for block in range(turned.shape[0]):
        proj = matmul(halves, turned[block])
        quads = []
        for k in range(count):
            shift = jnp.concatenate([shifts[k], shifts[k]], axis=1)
            off = proj[k * WIDTH : (k + 1) * WIDTH] - shift
            quads.append(jnp.sum(off * off, axis=0, keepdims=True))
        scores[block, :, :CELLS] = offsets - 0.5 * jnp.concatenate(quads, axis=0)
        scores[block, :, CELLS:] = centres


def likely_kernel(core, tile, part, mask, total, state, resp, near, far, means, totals):
    values = part[:, :CELLS]
    row = iotas((part.shape[0], WIDTH))[0]
    for n in range(2):
        own = jnp.where(row == 2 * tile[0] + n, part[:, CELLS:], 0.0)
        means[n : n + 1] = jnp.sum(own, axis=0, keepdims=True)
    tissue_f = mask[mask.shape[0] - 1 :]
    top = jnp.max(values, axis=0, keepdims=True)
    expon = jnp.exp(values - top)
    weight = jnp.sum(expon, axis=0, keepdims=True)
    first = expon / weight * tissue_f
    keep(values, first, tissue_f, state)
    put(core[0], first, resp, near, far)
    lse = jnp.sum((top + jnp.log(weight)) * tissue_f, axis=1, keepdims=True)
    cells = jnp.sum(tissue_f, axis=1, keepdims=True)
    lane = iotas((1, WIDTH))[1]
    result = jnp.where(lane == 0, lse, jnp.where(lane == 1, cells, total[...]))
    for n in range(totals.shape[0]):
        totals[n] = jnp.broadcast_to(result, totals.shape[1:])


def swap_all(value, axes):
    return lax.all_to_all(value, axes, 0, 0, tiled=True)


def swap_lines(value, groups):
    return lax.all_to_all(value, PLANE, 0, 0, axis_index_groups=groups, tiled=True)


def shards(embed, tissue, whiten0, means0, weights0):
    count = whiten0.shape[0]
    f32 = jnp.float32
    flat = embed.reshape(CELLS, WIDTH)
    core = lax.axis_index("core").reshape(1)
    tile = lax.axis_index(TILE).reshape(1)
    resp_shapes = [((count, CELLS), f32), ((count, WIDTH), f32), ((count, WIDTH), f32)]
    state_shape = ((2 * count + 8, CELLS), f32)

    before, resp, near, far, spread = start(
        core, weights0.reshape(1, count), flat, tissue.reshape(2, WIDTH), means0, whiten0
    )
    mine = swap_all(spread, BRICK[:2])
    kept_shape = ((count + 8, CELLS), f32)
    resp, near, far, kept = call(
        early_kernel, resp_shapes + [kept_shape], core, before, *halos(resp, near, far), scalars=1
    )
    resp, near, far, mine = lax.optimization_barrier((resp, near, far, mine))
    theirs = lax.ppermute(mine, "core", [(0, 1), (1, 0)])
    (resp,) = call(
        later_kernel, resp_shapes[:1], core, kept, resp, *halos(resp, near, far), scalars=1
    )
    resp, theirs = lax.optimization_barrier((resp, theirs))

    part = swap_all(resp.reshape(8, 8, CELLS), BRICK)
    packets, turned, total = call(
        moments_kernel,
        [((8, PACKET, WIDTH), f32), ((8, WIDTH, CELLS), jnp.bfloat16), ((1, WIDTH), f32)],
        core, part, mine, theirs, scalars=1, flops=1 << 30,
    )
    (packets,) = call(gather_kernel, [((8, PACKET, WIDTH), f32)], swap_lines(packets, NEAR))
    packets = swap_lines(packets, FAR)
    (packets,) = call(factor_kernel, [((8, PACKET, WIDTH), f32)], packets, flops=1 << 27)
    packets = swap_lines(packets, NEAR)
    (part,) = call(
        second_kernel, [((8, 8, CELLS + WIDTH), f32)], packets, turned, flops=1 << 29
    )
    part = swap_all(part, BRICK).reshape(count, CELLS + WIDTH)

    sizes = [lax.axis_size(axes) for axes in ROUND]
    state, resp, near, far, means_out, totals = call(
        likely_kernel,
        [state_shape] + resp_shapes + [((2, WIDTH), f32), ((sizes[0], 16, WIDTH), f32)],
        core, tile, part, kept, total, scalars=2,
    )
    totals = swap_all(totals, ROUND[0])
    resp, near, far = call(
        first_kernel, resp_shapes, core, state, *halos(resp, near, far), scalars=1
    )
    totals, resp, near, far = lax.optimization_barrier((totals, resp, near, far))
    totals = jnp.broadcast_to(jnp.sum(totals, axis=0)[None, :8], (sizes[1], 8, WIDTH))
    totals = swap_all(totals, ROUND[1])
    sides = halos(resp, near, far)
    resp_final, score = pl.pallas_call(
        last_kernel,
        out_shape=[
            jax.ShapeDtypeStruct((count, 2, WIDTH), f32), jax.ShapeDtypeStruct((1, 1), f32)
        ],
        in_specs=[SMEM] + [VMEM] * 7,
        out_specs=[VMEM, SMEM],
        compiler_params=PARAMS,
    )(core, state, resp, *sides, totals)
    return (resp_final.reshape(count, 1, 2, WIDTH), means_out, score.reshape(()))


def solution(mesh):
    bits = Mesh(mesh.devices.reshape((2,) * 9), SLAB + TILE)
    in_specs = (P(SLAB, TILE, None, None), P(SLAB, TILE, None), P(), P(), P())
    out_specs = (P(None, SLAB, TILE, None), P(TILE, None), P())
    return jax.shard_map(shards, mesh=bits, in_specs=in_specs, out_specs=out_specs, check_vma=False)
```

```python
import jax
import jax.numpy as jnp
from jax import lax
from jax.experimental import pallas as pl
from jax.experimental.pallas import tpu as pltpu
from jax.sharding import Mesh
from jax.sharding import PartitionSpec as P

SWEEPS = 2
BETA_POTTS = 1.0
COV_RIDGE = 0.01

SLAB = ("x1", "x0", "z2", "z1")
TILE = ("z0", "y2", "y1", "y0", "core")
BRICK = ("x1", "x0", "core")
PLANE = ("z2", "z1", "z0", "y2", "y1", "y0", "core")
ALONG_Y = [[[z * 16 + y * 2 + core for y in range(8)] for z in range(8)] for core in range(2)]
ALONG_Z = [[[z * 16 + y * 2 + core for z in range(8)] for y in range(8)] for core in range(2)]
NEAR = ALONG_Y[0] + ALONG_Z[1]
FAR = ALONG_Z[0] + ALONG_Y[1]
ROUND = (("y2", "y1", "y0", "core"), ("x1", "x0", "z2", "z1", "z0"))

WIDTH = 128
CELLS = 256
DEVICES = 512
HALF = 64
PACKET = HALF + 8
VMEM = pl.BlockSpec(memory_space=pltpu.VMEM)
SMEM = pl.BlockSpec(memory_space=pltpu.SMEM)
HBM = pl.BlockSpec(memory_space=pl.ANY)
PARAMS = pltpu.CompilerParams(vmem_limit_bytes=40 * 1024 * 1024)


def call(kernel, shapes, *args, scalars=0, flops=1 << 20):
    out = [jax.ShapeDtypeStruct(shape, kind) for shape, kind in shapes]
    return pl.pallas_call(
        kernel,
        out_shape=out,
        in_specs=[SMEM] * scalars + [VMEM] * (len(args) - scalars),
        out_specs=[VMEM] * len(out),
        compiler_params=PARAMS,
        cost_estimate=pl.CostEstimate(flops=flops, bytes_accessed=1 << 20, transcendentals=0),
    )(*args)


def iotas(shape):
    return (
        lax.broadcasted_iota(jnp.int32, shape, 0),
        lax.broadcasted_iota(jnp.int32, shape, 1),
    )


def matmul(lhs, rhs, dims=((1,), (0,))):
    return lax.dot_general(lhs, rhs, (dims, ((), ())), preferred_element_type=jnp.float32)


def normalise(scores):
    top = jnp.max(scores, axis=0, keepdims=True)
    expon = jnp.exp(scores - top)
    return expon / jnp.sum(expon, axis=0, keepdims=True)


def keep(scores, resp, mask, state):
    count = scores.shape[0]
    state[:count] = scores
    state[count : 2 * count] = resp
    state[2 * count :] = jnp.broadcast_to(mask, (state.shape[0] - 2 * count, CELLS))


def put(core, resp, resp_ref, near_ref, far_ref):
    first, last = resp[:, :WIDTH], resp[:, WIDTH:]
    resp_ref[...] = resp
    near_ref[...] = jnp.where(core == 0, last, first)
    far_ref[...] = jnp.where(core == 0, first, last)


CHUNK = 16


def start_kernel(
    core, weights, flat, tissue, means, whiten,
    state, resp, near, far, spread,
    weights_in, flat_in, tissue_in, means_in, whiten_in, diag, sems,
):
    count = whiten.shape[0]
    small = zip((flat, means, tissue, weights), (flat_in, means_in, tissue_in, weights_in))
    copies = [pltpu.make_async_copy(src, dst, sems.at[n]) for n, (src, dst) in enumerate(small)]
    blocks = [
        pltpu.make_async_copy(
            whiten.at[pl.ds(begin, CHUNK)],
            whiten_in.at[pl.ds(begin, CHUNK)],
            sems.at[4 + begin // CHUNK],
        )
        for begin in range(0, count, CHUNK)
    ]
    for copy in copies + blocks:
        copy.start()
    row_at, col_at = iotas((WIDTH, WIDTH))
    copies[0].wait()
    full = flat_in[...].astype(jnp.float32)
    cells = full.T.astype(jnp.bfloat16)
    for n in range(spread.shape[0]):
        spread[n] = full
    for copy in copies[1:]:
        copy.wait()
    for n, block in enumerate(blocks):
        block.wait()
        for own in range(n * CHUNK, (n + 1) * CHUNK):
            matrix = whiten_in[own]
            full = matrix.astype(jnp.float32)
            shift = jnp.sum(full * means_in[own : own + 1], axis=1, keepdims=True)
            proj = matmul(matrix, cells) - shift
            state[own : own + 1] = jnp.sum(proj * proj, axis=0, keepdims=True)
            diag[own : own + 1] = jnp.sum(
                jnp.where(row_at == col_at, full, 0.0), axis=0, keepdims=True
            )
    prior = weights_in[...]
    prior = jnp.log(prior / jnp.sum(prior, axis=1, keepdims=True))
    row_at, col_at = iotas((count, count))
    prior = jnp.where(row_at == col_at, jnp.broadcast_to(prior, (count, count)), 0.0)
    offset = jnp.sum(prior, axis=1, keepdims=True) + jnp.sum(
        jnp.log(diag[...]), axis=1, keepdims=True
    )
    result = offset - 0.5 * state[:count]
    tissue_f = tissue_in[...].astype(jnp.float32)
    tissue_f = jnp.concatenate([tissue_f[:1], tissue_f[1:]], axis=1)
    first = normalise(result) * tissue_f
    keep(result, first, tissue_f, state)
    put(core[0], first, resp, near, far)


def start(core, weights, flat, tissue, means, whiten):
    count = whiten.shape[0]
    f32 = jnp.float32
    shapes = [(2 * count + 8, CELLS), (count, CELLS), (count, WIDTH), (count, WIDTH)]
    shapes += [(4, CELLS, WIDTH)]
    return pl.pallas_call(
        start_kernel,
        out_shape=[jax.ShapeDtypeStruct(shape, f32) for shape in shapes],
        in_specs=[SMEM] + [HBM] * 5,
        out_specs=[VMEM] * len(shapes),
        scratch_shapes=[
            pltpu.VMEM(weights.shape, f32),
            pltpu.VMEM(flat.shape, flat.dtype),
            pltpu.VMEM(tissue.shape, tissue.dtype),
            pltpu.VMEM(means.shape, f32),
            pltpu.VMEM(whiten.shape, whiten.dtype),
            pltpu.VMEM((count, WIDTH), f32),
            pltpu.SemaphoreType.DMA((4 + count // CHUNK,)),
        ],
        compiler_params=pltpu.CompilerParams(vmem_limit_bytes=58 * 1024 * 1024),
        cost_estimate=pl.CostEstimate(flops=1 << 29, bytes_accessed=1 << 21, transcendentals=0),
    )(core, weights, flat, tissue, means, whiten)


def swept(core, state, resp, slab_even, slab_odd, far_in, near_in):
    count = resp.shape[0]
    lane = iotas((count, WIDTH))[1]
    rows = (resp[:, :WIDTH], resp[:, WIDTH:])
    below = jnp.where(core[0] == 0, far_in[...], near_in[...])
    above = jnp.where(core[0] == 0, near_in[...], far_in[...])
    fields = []
    for row, others in zip(rows, (below + rows[1], rows[0] + above)):
        after = jnp.where(lane < WIDTH - 1, pltpu.roll(row, WIDTH - 1, 1), 0.0)
        before = jnp.where(lane > 0, pltpu.roll(row, 1, 1), 0.0)
        fields.append(others + after + before)
    field = jnp.concatenate(fields, axis=1) + slab_even[...] + slab_odd[...]
    scores, mask = state[:count], state[state.shape[0] - 1 :]
    return normalise(scores + BETA_POTTS * field) * mask


def first_kernel(core, state, slab_even, slab_odd, far_in, near_in, out, near, far):
    count = out.shape[0]
    resp = state[count : 2 * count]
    put(core[0], swept(core, state, resp, slab_even, slab_odd, far_in, near_in), out, near, far)


def early_kernel(core, state, slab_even, slab_odd, far_in, near_in, out, near, far, kept):
    count = out.shape[0]
    kept[:count] = state[:count]
    kept[count:] = state[2 * count :]
    first_kernel(core, state, slab_even, slab_odd, far_in, near_in, out, near, far)


def middle_kernel(
    core, state, slab_even, slab_odd, far_in, near_in, totals, out, near, far, sums
):
    total = totals[0]
    for n in range(1, totals.shape[0]):
        total = total + totals[n]
    for n in range(sums.shape[0]):
        sums[n] = total[: sums.shape[1]]
    first_kernel(core, state, slab_even, slab_odd, far_in, near_in, out, near, far)


def later_kernel(core, state, resp, slab_even, slab_odd, far_in, near_in, out):
    out[...] = swept(core, state, resp[...], slab_even, slab_odd, far_in, near_in)


def last_kernel(core, state, resp, slab_even, slab_odd, far_in, near_in, totals, out, score):
    result = swept(core, state, resp[...], slab_even, slab_odd, far_in, near_in)
    out[:, 0, :] = result[:, :WIDTH]
    out[:, 1, :] = result[:, WIDTH:]
    total = totals[0]
    for n in range(1, totals.shape[0]):
        total = total + totals[n]
    total = total[:1]
    lane = iotas((1, WIDTH))[1]
    lse = jnp.sum(jnp.where(lane == 0, total, 0.0))
    level = jnp.sum(jnp.where(lane == 2, jnp.log(total), 0.0))
    cells = jnp.sum(jnp.where(lane == 1, total, 0.0))
    score[0, 0] = (lse - cells * level) / (CELLS * DEVICES)


def swapped(part, axes, begin):
    count = lax.axis_size(axes)
    pairs = [(i, i + 1) for i in range(begin, count - 1, 2)]
    return lax.ppermute(part, axes, pairs + [(j, i) for i, j in pairs])


def halos(resp, near, far):
    return (
        swapped(resp, SLAB, 0), swapped(resp, SLAB, 1), swapped(far, TILE, 1), swapped(near, TILE, 0)
    )


def moments_kernel(core, resp, mine, theirs, packet, turned, total):
    blocks, count = resp.shape[:2]
    row_at, col_at = iotas((WIDTH, WIDTH))
    ones = jnp.ones((CELLS, WIDTH), jnp.bfloat16)
    acc = [jnp.zeros((WIDTH, 2 * WIDTH), jnp.float32) for _ in range(count)]
    for n in range(blocks):
        cells = mine[n // 2] if n % 2 == 0 else theirs[n // 2]
        block = n + core[0] if n % 2 == 0 else n - core[0]
        weight = resp[block]
        flipped = cells.T
        turned[block] = flipped.astype(jnp.bfloat16)
        wide = jnp.concatenate([cells.astype(jnp.bfloat16), ones], axis=1)
        for k in range(count):
            weighted = (flipped * weight[k : k + 1]).astype(jnp.bfloat16)
            acc[k] = acc[k] + matmul(weighted, wide)
    firsts = jnp.zeros((WIDTH, WIDTH), jnp.float32)
    for k in range(count):
        firsts = jnp.where(col_at == k, acc[k][:, WIDTH:], firsts)
    firsts = firsts.T
    counts = jnp.sum(jnp.sum(resp[...], axis=0), axis=1, keepdims=True)
    counts = jnp.broadcast_to(counts, (count, WIDTH))
    total[...] = jnp.sum(counts, axis=0, keepdims=True)
    fold_row, fold_col = iotas((HALF, WIDTH))
    for k in range(count):
        sym = acc[k][:, :WIDTH]
        sym = sym + sym.T
        low = (fold_col < HALF) | (fold_row > fold_col - HALF)
        packet[k, :HALF] = jnp.where(low, sym[HALF:], pltpu.roll(sym[:HALF], HALF, 1))
        diag = jnp.sum(jnp.where(row_at == col_at, sym, 0.0), axis=0, keepdims=True)
        packet[k, HALF:] = jnp.concatenate(
            [diag, firsts[k : k + 1], counts[k : k + 1], jnp.zeros((5, WIDTH), jnp.float32)],
            axis=0,
        )


def gather_kernel(packets, out):
    total = jnp.sum(packets[...], axis=0)
    for k in range(out.shape[0]):
        out[k] = total


def split(value):
    high = value.astype(jnp.bfloat16).astype(jnp.float32)
    rest = value - high
    middle = rest.astype(jnp.bfloat16).astype(jnp.float32)
    return high, middle, rest - middle


STEP = 16


def whiten_chain(cov):
    row_at, col_at = iotas((WIDTH, WIDTH))
    wide = (STEP, 2 * WIDTH)
    rest = jnp.concatenate([cov, jnp.where(row_at == col_at, 1.0, 0.0)], axis=1)
    sub = lax.broadcasted_iota(jnp.int32, (STEP, WIDTH), 0)
    done, scales = [], []
    for begin in range(0, WIDTH, STEP):
        panel = rest[:STEP]
        cols = [
            jnp.broadcast_to(panel[:, begin + j : begin + j + 1], (STEP, WIDTH))
            for j in range(STEP)
        ]
        scale = jnp.broadcast_to(cols[0][:1], (STEP, WIDTH))
        for j in range(STEP - 1):
            inverse = lax.rsqrt(cols[j][j : j + 1])
            inverse = inverse * inverse
            mult = jnp.where(sub > j, cols[j] * inverse, 0.0)
            for l in range(j + 1, STEP):
                cols[l] = cols[l] - mult * jnp.broadcast_to(cols[l][j : j + 1], (STEP, WIDTH))
            both = jnp.concatenate([mult, mult], axis=1)
            panel = panel - both * jnp.broadcast_to(panel[j : j + 1], wide)
            pivot = jnp.broadcast_to(cols[j + 1][j + 1 : j + 2], (STEP, WIDTH))
            scale = jnp.where(sub > j, pivot, scale)
        root = lax.rsqrt(scale)
        panel = panel * jnp.concatenate([root, root], axis=1)
        scales.append(scale)
        done.append(panel[:, WIDTH:])
        if begin + STEP < WIDTH:
            high, middle, low = split(panel)
            right = jnp.concatenate([high, middle, low, high, middle, high], axis=0)
            high, middle, low = (part[:, :WIDTH] for part in (high, middle, low))
            left = jnp.concatenate([high, high, high, middle, middle, low], axis=0)
            update = matmul(left.astype(jnp.bfloat16), right.astype(jnp.bfloat16), ((0,), (0,)))
            rest = rest[STEP:] - update[begin + STEP :]
    logdet = -0.5 * jnp.sum(jnp.log(jnp.concatenate(scales, axis=0)), axis=0, keepdims=True)
    return jnp.concatenate(done, axis=0), logdet


def unfolded(fold):
    both = jnp.concatenate([pltpu.roll(fold, HALF, 1), fold], axis=0)
    return both, both.T


def factor_kernel(packets, out):
    row_at, col_at = iotas((WIDTH, WIDTH))
    packet = jnp.sum(packets[...], axis=0)
    both, turned = unfolded(packet[:HALF])
    diag, first, counts = (packet[HALF + n : HALF + n + 1] for n in range(3))
    left = col_at < HALF
    kept = (left & (row_at <= col_at)) | ((row_at >= HALF) & (left | (row_at > col_at)))
    sym = jnp.where(row_at == col_at, diag, jnp.where(kept, both, turned))
    centre = first / counts
    tall = jnp.broadcast_to(centre, (WIDTH, WIDTH))
    cov = 0.5 * sym / counts - tall.T * tall
    cov = jnp.where(row_at == col_at, cov + COV_RIDGE, cov)
    whiten, logdet = whiten_chain(cov)
    shift = jnp.sum(whiten * tall, axis=1, keepdims=True)
    shift = jnp.broadcast_to(shift, (WIDTH, WIDTH)).T[:1]
    offset = jnp.log(counts) + logdet
    diag = jnp.sum(jnp.where(row_at == col_at, whiten, 0.0), axis=0, keepdims=True)
    fold_row, fold_col = iotas((HALF, WIDTH))
    low = (fold_col < HALF) | (fold_row >= fold_col - HALF)
    fold = jnp.where(low, whiten[HALF:], pltpu.roll(whiten.T[:HALF], HALF, 1))
    zeros = jnp.zeros((4, WIDTH), jnp.float32)
    result = jnp.concatenate([fold, diag, shift, centre, offset, zeros], axis=0)
    for k in range(out.shape[0]):
        out[k] = result


def second_kernel(packets, turned, scores):
    row_at, col_at = iotas((WIDTH, WIDTH))
    top, left = row_at < HALF, col_at < HALF
    below = (row_at >= HALF) & (left | (row_at >= col_at))
    above = top & (row_at > col_at)
    count = packets.shape[0]
    halves, shifts, offsets, centres = [], [], [], []
    for k in range(count):
        both, flipped = unfolded(packets[k, :HALF])
        diag, shift, centre, offset = (packets[k, HALF + n : HALF + n + 1] for n in range(4))
        whiten = jnp.where(below, both, jnp.where(above, flipped, 0.0))
        whiten = jnp.where(top & (row_at == col_at), diag, whiten)
        halves.append(whiten.astype(jnp.bfloat16))
        shifts.append(jnp.broadcast_to(shift, (WIDTH, WIDTH)).T)
        offsets.append(offset)
        centres.append(centre)
    halves = jnp.concatenate(halves, axis=0)
    offsets = jnp.concatenate(offsets, axis=0)
    offsets = jnp.concatenate([offsets, offsets], axis=1)
    centres = jnp.concatenate(centres, axis=0)
    for block in range(turned.shape[0]):
        proj = matmul(halves, turned[block])
        quads = []
        for k in range(count):
            shift = jnp.concatenate([shifts[k], shifts[k]], axis=1)
            off = proj[k * WIDTH : (k + 1) * WIDTH] - shift
            quads.append(jnp.sum(off * off, axis=0, keepdims=True))
        scores[block, :, :CELLS] = offsets - 0.5 * jnp.concatenate(quads, axis=0)
        scores[block, :, CELLS:] = centres


def likely_kernel(core, tile, part, mask, total, state, resp, near, far, means, totals):
    values = part[:, :CELLS]
    row = iotas((part.shape[0], WIDTH))[0]
    for n in range(2):
        own = jnp.where(row == 2 * tile[0] + n, part[:, CELLS:], 0.0)
        means[n : n + 1] = jnp.sum(own, axis=0, keepdims=True)
    tissue_f = mask[mask.shape[0] - 1 :]
    top = jnp.max(values, axis=0, keepdims=True)
    expon = jnp.exp(values - top)
    weight = jnp.sum(expon, axis=0, keepdims=True)
    first = expon / weight * tissue_f
    keep(values, first, tissue_f, state)
    put(core[0], first, resp, near, far)
    lse = jnp.sum((top + jnp.log(weight)) * tissue_f, axis=1, keepdims=True)
    cells = jnp.sum(tissue_f, axis=1, keepdims=True)
    lane = iotas((1, WIDTH))[1]
    result = jnp.where(lane == 0, lse, jnp.where(lane == 1, cells, total[...]))
    for n in range(totals.shape[0]):
        totals[n] = jnp.broadcast_to(result, totals.shape[1:])


def swap_all(value, axes):
    return lax.all_to_all(value, axes, 0, 0, tiled=True)


def swap_lines(value, groups):
    return lax.all_to_all(value, PLANE, 0, 0, axis_index_groups=groups, tiled=True)


def shards(embed, tissue, whiten0, means0, weights0):
    count = whiten0.shape[0]
    f32 = jnp.float32
    flat = embed.reshape(CELLS, WIDTH)
    core = lax.axis_index("core").reshape(1)
    tile = lax.axis_index(TILE).reshape(1)
    resp_shapes = [((count, CELLS), f32), ((count, WIDTH), f32), ((count, WIDTH), f32)]
    state_shape = ((2 * count + 8, CELLS), f32)

    before, resp, near, far, spread = start(
        core, weights0.reshape(1, count), flat, tissue.reshape(2, WIDTH), means0, whiten0
    )
    mine = swap_all(spread, BRICK[:2])
    kept_shape = ((count + 8, CELLS), f32)
    resp, near, far, kept = call(
        early_kernel, resp_shapes + [kept_shape], core, before, *halos(resp, near, far), scalars=1
    )
    resp, near, far, mine = lax.optimization_barrier((resp, near, far, mine))
    theirs = lax.ppermute(mine, "core", [(0, 1), (1, 0)])
    (resp,) = call(
        later_kernel, resp_shapes[:1], core, kept, resp, *halos(resp, near, far), scalars=1
    )
    resp, theirs = lax.optimization_barrier((resp, theirs))

    part = swap_all(resp.reshape(8, 8, CELLS), BRICK)
    packets, turned, total = call(
        moments_kernel,
        [((8, PACKET, WIDTH), f32), ((8, WIDTH, CELLS), jnp.bfloat16), ((1, WIDTH), f32)],
        core, part, mine, theirs, scalars=1, flops=1 << 30,
    )
    (packets,) = call(gather_kernel, [((8, PACKET, WIDTH), f32)], swap_lines(packets, NEAR))
    packets = swap_lines(packets, FAR)
    (packets,) = call(factor_kernel, [((8, PACKET, WIDTH), f32)], packets, flops=1 << 27)
    packets = swap_lines(packets, NEAR)
    (part,) = call(
        second_kernel, [((8, 8, CELLS + WIDTH), f32)], packets, turned, flops=1 << 29
    )
    part = swap_all(part, BRICK).reshape(count, CELLS + WIDTH)

    sizes = [lax.axis_size(axes) for axes in ROUND]
    state, resp, near, far, means_out, totals = call(
        likely_kernel,
        [state_shape] + resp_shapes + [((2, WIDTH), f32), ((sizes[0], 16, WIDTH), f32)],
        core, tile, part, kept, total, scalars=2,
    )
    totals = swap_all(totals, ROUND[0])
    resp, near, far, totals = call(
        middle_kernel, resp_shapes + [((sizes[1], 8, WIDTH), f32)],
        core, state, *halos(resp, near, far), totals, scalars=1,
    )
    totals = swap_all(totals, ROUND[1])
    sides = halos(resp, near, far)
    resp_final, score = pl.pallas_call(
        last_kernel,
        out_shape=[
            jax.ShapeDtypeStruct((count, 2, WIDTH), f32), jax.ShapeDtypeStruct((1, 1), f32)
        ],
        in_specs=[SMEM] + [VMEM] * 7,
        out_specs=[VMEM, SMEM],
        compiler_params=PARAMS,
    )(core, state, resp, *sides, totals)
    return (resp_final.reshape(count, 1, 2, WIDTH), means_out, score.reshape(()))


def solution(mesh):
    bits = Mesh(mesh.devices.reshape((2,) * 9), SLAB + TILE)
    in_specs = (P(SLAB, TILE, None, None), P(SLAB, TILE, None), P(), P(), P())
    out_specs = (P(None, SLAB, TILE, None), P(TILE, None), P())
    return jax.shard_map(shards, mesh=bits, in_specs=in_specs, out_specs=out_specs, check_vma=False)
```

```python
import jax
import jax.numpy as jnp
from jax import lax
from jax.experimental import pallas as pl
from jax.experimental.pallas import tpu as pltpu
from jax.sharding import Mesh
from jax.sharding import PartitionSpec as P

SWEEPS = 2
BETA_POTTS = 1.0
COV_RIDGE = 0.01

SLAB = ("x1", "x0", "z2", "z1")
TILE = ("z0", "y2", "y1", "y0", "core")
BRICK = ("x1", "x0", "core")
PLANE = ("z2", "z1", "z0", "y2", "y1", "y0", "core")
ALONG_Y = [[[z * 16 + y * 2 + core for y in range(8)] for z in range(8)] for core in range(2)]
ALONG_Z = [[[z * 16 + y * 2 + core for z in range(8)] for y in range(8)] for core in range(2)]
NEAR = ALONG_Y[0] + ALONG_Z[1]
FAR = ALONG_Z[0] + ALONG_Y[1]
ROUND = (("y2", "y1", "y0", "core"), ("x1", "x0", "z2", "z1", "z0"))

WIDTH = 128
CELLS = 256
DEVICES = 512
HALF = 64
PACKET = HALF + 8
VMEM = pl.BlockSpec(memory_space=pltpu.VMEM)
SMEM = pl.BlockSpec(memory_space=pltpu.SMEM)
HBM = pl.BlockSpec(memory_space=pl.ANY)
PARAMS = pltpu.CompilerParams(vmem_limit_bytes=40 * 1024 * 1024)


def call(kernel, shapes, *args, scalars=0, flops=1 << 20):
    out = [jax.ShapeDtypeStruct(shape, kind) for shape, kind in shapes]
    return pl.pallas_call(
        kernel,
        out_shape=out,
        in_specs=[SMEM] * scalars + [VMEM] * (len(args) - scalars),
        out_specs=[VMEM] * len(out),
        compiler_params=PARAMS,
        cost_estimate=pl.CostEstimate(flops=flops, bytes_accessed=1 << 20, transcendentals=0),
    )(*args)


def iotas(shape):
    return (
        lax.broadcasted_iota(jnp.int32, shape, 0),
        lax.broadcasted_iota(jnp.int32, shape, 1),
    )


def matmul(lhs, rhs, dims=((1,), (0,))):
    return lax.dot_general(lhs, rhs, (dims, ((), ())), preferred_element_type=jnp.float32)


def normalise(scores):
    top = jnp.max(scores, axis=0, keepdims=True)
    expon = jnp.exp(scores - top)
    return expon / jnp.sum(expon, axis=0, keepdims=True)


def keep(scores, resp, mask, state):
    count = scores.shape[0]
    state[:count] = scores
    state[count : 2 * count] = resp
    state[2 * count :] = jnp.broadcast_to(mask, (state.shape[0] - 2 * count, CELLS))


def put(core, resp, resp_ref, near_ref, far_ref):
    first, last = resp[:, :WIDTH], resp[:, WIDTH:]
    resp_ref[...] = resp
    near_ref[...] = jnp.where(core == 0, last, first)
    far_ref[...] = jnp.where(core == 0, first, last)


CHUNK = 16


def start_kernel(
    core, weights, flat, tissue, means, whiten,
    state, resp, near, far, spread,
    weights_in, flat_in, tissue_in, means_in, whiten_in, diag, sems,
):
    count = whiten.shape[0]
    small = zip((flat, means, tissue, weights), (flat_in, means_in, tissue_in, weights_in))
    copies = [pltpu.make_async_copy(src, dst, sems.at[n]) for n, (src, dst) in enumerate(small)]
    blocks = [
        pltpu.make_async_copy(
            whiten.at[pl.ds(begin, CHUNK)],
            whiten_in.at[pl.ds(begin, CHUNK)],
            sems.at[4 + begin // CHUNK],
        )
        for begin in range(0, count, CHUNK)
    ]
    for copy in copies + blocks:
        copy.start()
    row_at, col_at = iotas((WIDTH, WIDTH))
    copies[0].wait()
    full = flat_in[...].astype(jnp.float32)
    cells = full.T.astype(jnp.bfloat16)
    for n in range(spread.shape[0]):
        spread[n] = full
    for copy in copies[1:]:
        copy.wait()
    for n, block in enumerate(blocks):
        block.wait()
        for own in range(n * CHUNK, (n + 1) * CHUNK):
            matrix = whiten_in[own]
            full = matrix.astype(jnp.float32)
            shift = jnp.sum(full * means_in[own : own + 1], axis=1, keepdims=True)
            proj = matmul(matrix, cells) - shift
            state[own : own + 1] = jnp.sum(proj * proj, axis=0, keepdims=True)
            diag[own : own + 1] = jnp.sum(
                jnp.where(row_at == col_at, full, 0.0), axis=0, keepdims=True
            )
    prior = weights_in[...]
    prior = jnp.log(prior / jnp.sum(prior, axis=1, keepdims=True))
    row_at, col_at = iotas((count, count))
    prior = jnp.where(row_at == col_at, jnp.broadcast_to(prior, (count, count)), 0.0)
    offset = jnp.sum(prior, axis=1, keepdims=True) + jnp.sum(
        jnp.log(diag[...]), axis=1, keepdims=True
    )
    result = offset - 0.5 * state[:count]
    tissue_f = tissue_in[...].astype(jnp.float32)
    tissue_f = jnp.concatenate([tissue_f[:1], tissue_f[1:]], axis=1)
    first = normalise(result) * tissue_f
    keep(result, first, tissue_f, state)
    put(core[0], first, resp, near, far)


def start(core, weights, flat, tissue, means, whiten):
    count = whiten.shape[0]
    f32 = jnp.float32
    shapes = [(2 * count + 8, CELLS), (count, CELLS), (count, WIDTH), (count, WIDTH)]
    shapes += [(8, CELLS, WIDTH)]
    return pl.pallas_call(
        start_kernel,
        out_shape=[jax.ShapeDtypeStruct(shape, f32) for shape in shapes],
        in_specs=[SMEM] + [HBM] * 5,
        out_specs=[VMEM] * len(shapes),
        scratch_shapes=[
            pltpu.VMEM(weights.shape, f32),
            pltpu.VMEM(flat.shape, flat.dtype),
            pltpu.VMEM(tissue.shape, tissue.dtype),
            pltpu.VMEM(means.shape, f32),
            pltpu.VMEM(whiten.shape, whiten.dtype),
            pltpu.VMEM((count, WIDTH), f32),
            pltpu.SemaphoreType.DMA((4 + count // CHUNK,)),
        ],
        compiler_params=pltpu.CompilerParams(vmem_limit_bytes=58 * 1024 * 1024),
        cost_estimate=pl.CostEstimate(flops=1 << 29, bytes_accessed=1 << 21, transcendentals=0),
    )(core, weights, flat, tissue, means, whiten)


def swept(core, state, resp, slab_even, slab_odd, far_in, near_in):
    count = resp.shape[0]
    lane = iotas((count, WIDTH))[1]
    rows = (resp[:, :WIDTH], resp[:, WIDTH:])
    below = jnp.where(core[0] == 0, far_in[...], near_in[...])
    above = jnp.where(core[0] == 0, near_in[...], far_in[...])
    fields = []
    for row, others in zip(rows, (below + rows[1], rows[0] + above)):
        after = jnp.where(lane < WIDTH - 1, pltpu.roll(row, WIDTH - 1, 1), 0.0)
        before = jnp.where(lane > 0, pltpu.roll(row, 1, 1), 0.0)
        fields.append(others + after + before)
    field = jnp.concatenate(fields, axis=1) + slab_even[...] + slab_odd[...]
    scores, mask = state[:count], state[state.shape[0] - 1 :]
    return normalise(scores + BETA_POTTS * field) * mask


def first_kernel(core, state, slab_even, slab_odd, far_in, near_in, out, near, far):
    count = out.shape[0]
    resp = state[count : 2 * count]
    put(core[0], swept(core, state, resp, slab_even, slab_odd, far_in, near_in), out, near, far)


def early_kernel(core, state, slab_even, slab_odd, far_in, near_in, out, near, far, kept):
    count = out.shape[0]
    kept[:count] = state[:count]
    kept[count:] = state[2 * count :]
    first_kernel(core, state, slab_even, slab_odd, far_in, near_in, out, near, far)


def middle_kernel(
    core, state, slab_even, slab_odd, far_in, near_in, totals, out, near, far, sums
):
    total = totals[0]
    for n in range(1, totals.shape[0]):
        total = total + totals[n]
    for n in range(sums.shape[0]):
        sums[n] = total[: sums.shape[1]]
    first_kernel(core, state, slab_even, slab_odd, far_in, near_in, out, near, far)


def later_kernel(core, state, resp, slab_even, slab_odd, far_in, near_in, out):
    out[...] = swept(core, state, resp[...], slab_even, slab_odd, far_in, near_in)


def last_kernel(core, state, resp, slab_even, slab_odd, far_in, near_in, totals, out, score):
    result = swept(core, state, resp[...], slab_even, slab_odd, far_in, near_in)
    out[:, 0, :] = result[:, :WIDTH]
    out[:, 1, :] = result[:, WIDTH:]
    total = totals[0]
    for n in range(1, totals.shape[0]):
        total = total + totals[n]
    total = total[:1]
    lane = iotas((1, WIDTH))[1]
    lse = jnp.sum(jnp.where(lane == 0, total, 0.0))
    level = jnp.sum(jnp.where(lane == 2, jnp.log(total), 0.0))
    cells = jnp.sum(jnp.where(lane == 1, total, 0.0))
    score[0, 0] = (lse - cells * level) / (CELLS * DEVICES)


def swapped(part, axes, begin):
    count = lax.axis_size(axes)
    pairs = [(i, i + 1) for i in range(begin, count - 1, 2)]
    return lax.ppermute(part, axes, pairs + [(j, i) for i, j in pairs])


def halos(resp, near, far):
    return (
        swapped(resp, SLAB, 0), swapped(resp, SLAB, 1), swapped(far, TILE, 1), swapped(near, TILE, 0)
    )


def moments_kernel(resp, shared, packet, turned, total):
    blocks, count = resp.shape[:2]
    row_at, col_at = iotas((WIDTH, WIDTH))
    ones = jnp.ones((CELLS, WIDTH), jnp.bfloat16)
    acc = [jnp.zeros((WIDTH, 2 * WIDTH), jnp.float32) for _ in range(count)]
    for block in range(blocks):
        cells, weight = shared[block], resp[block]
        flipped = cells.T
        turned[block] = flipped.astype(jnp.bfloat16)
        wide = jnp.concatenate([cells.astype(jnp.bfloat16), ones], axis=1)
        for k in range(count):
            weighted = (flipped * weight[k : k + 1]).astype(jnp.bfloat16)
            acc[k] = acc[k] + matmul(weighted, wide)
    firsts = jnp.zeros((WIDTH, WIDTH), jnp.float32)
    for k in range(count):
        firsts = jnp.where(col_at == k, acc[k][:, WIDTH:], firsts)
    firsts = firsts.T
    counts = jnp.sum(jnp.sum(resp[...], axis=0), axis=1, keepdims=True)
    counts = jnp.broadcast_to(counts, (count, WIDTH))
    total[...] = jnp.sum(counts, axis=0, keepdims=True)
    fold_row, fold_col = iotas((HALF, WIDTH))
    for k in range(count):
        sym = acc[k][:, :WIDTH]
        sym = sym + sym.T
        low = (fold_col < HALF) | (fold_row > fold_col - HALF)
        packet[k, :HALF] = jnp.where(low, sym[HALF:], pltpu.roll(sym[:HALF], HALF, 1))
        diag = jnp.sum(jnp.where(row_at == col_at, sym, 0.0), axis=0, keepdims=True)
        packet[k, HALF:] = jnp.concatenate(
            [diag, firsts[k : k + 1], counts[k : k + 1], jnp.zeros((5, WIDTH), jnp.float32)],
            axis=0,
        )


def gather_kernel(packets, out):
    total = jnp.sum(packets[...], axis=0)
    for k in range(out.shape[0]):
        out[k] = total


def split(value):
    high = value.astype(jnp.bfloat16).astype(jnp.float32)
    rest = value - high
    middle = rest.astype(jnp.bfloat16).astype(jnp.float32)
    return high, middle, rest - middle


STEP = 16


def whiten_chain(cov):
    row_at, col_at = iotas((WIDTH, WIDTH))
    wide = (STEP, 2 * WIDTH)
    rest = jnp.concatenate([cov, jnp.where(row_at == col_at, 1.0, 0.0)], axis=1)
    sub = lax.broadcasted_iota(jnp.int32, (STEP, WIDTH), 0)
    done, scales = [], []
    for begin in range(0, WIDTH, STEP):
        panel = rest[:STEP]
        cols = [
            jnp.broadcast_to(panel[:, begin + j : begin + j + 1], (STEP, WIDTH))
            for j in range(STEP)
        ]
        scale = jnp.broadcast_to(cols[0][:1], (STEP, WIDTH))
        for j in range(STEP - 1):
            inverse = lax.rsqrt(cols[j][j : j + 1])
            inverse = inverse * inverse
            mult = jnp.where(sub > j, cols[j] * inverse, 0.0)
            for l in range(j + 1, STEP):
                cols[l] = cols[l] - mult * jnp.broadcast_to(cols[l][j : j + 1], (STEP, WIDTH))
            both = jnp.concatenate([mult, mult], axis=1)
            panel = panel - both * jnp.broadcast_to(panel[j : j + 1], wide)
            pivot = jnp.broadcast_to(cols[j + 1][j + 1 : j + 2], (STEP, WIDTH))
            scale = jnp.where(sub > j, pivot, scale)
        root = lax.rsqrt(scale)
        panel = panel * jnp.concatenate([root, root], axis=1)
        scales.append(scale)
        done.append(panel[:, WIDTH:])
        if begin + STEP < WIDTH:
            high, middle, low = split(panel)
            right = jnp.concatenate([high, middle, low, high, middle, high], axis=0)
            high, middle, low = (part[:, :WIDTH] for part in (high, middle, low))
            left = jnp.concatenate([high, high, high, middle, middle, low], axis=0)
            update = matmul(left.astype(jnp.bfloat16), right.astype(jnp.bfloat16), ((0,), (0,)))
            rest = rest[STEP:] - update[begin + STEP :]
    logdet = -0.5 * jnp.sum(jnp.log(jnp.concatenate(scales, axis=0)), axis=0, keepdims=True)
    return jnp.concatenate(done, axis=0), logdet


def unfolded(fold):
    both = jnp.concatenate([pltpu.roll(fold, HALF, 1), fold], axis=0)
    return both, both.T


def factor_kernel(packets, out):
    row_at, col_at = iotas((WIDTH, WIDTH))
    packet = jnp.sum(packets[...], axis=0)
    both, turned = unfolded(packet[:HALF])
    diag, first, counts = (packet[HALF + n : HALF + n + 1] for n in range(3))
    left = col_at < HALF
    kept = (left & (row_at <= col_at)) | ((row_at >= HALF) & (left | (row_at > col_at)))
    sym = jnp.where(row_at == col_at, diag, jnp.where(kept, both, turned))
    centre = first / counts
    tall = jnp.broadcast_to(centre, (WIDTH, WIDTH))
    cov = 0.5 * sym / counts - tall.T * tall
    cov = jnp.where(row_at == col_at, cov + COV_RIDGE, cov)
    whiten, logdet = whiten_chain(cov)
    shift = jnp.sum(whiten * tall, axis=1, keepdims=True)
    shift = jnp.broadcast_to(shift, (WIDTH, WIDTH)).T[:1]
    offset = jnp.log(counts) + logdet
    diag = jnp.sum(jnp.where(row_at == col_at, whiten, 0.0), axis=0, keepdims=True)
    fold_row, fold_col = iotas((HALF, WIDTH))
    low = (fold_col < HALF) | (fold_row >= fold_col - HALF)
    fold = jnp.where(low, whiten[HALF:], pltpu.roll(whiten.T[:HALF], HALF, 1))
    zeros = jnp.zeros((4, WIDTH), jnp.float32)
    result = jnp.concatenate([fold, diag, shift, centre, offset, zeros], axis=0)
    for k in range(out.shape[0]):
        out[k] = result


def second_kernel(packets, turned, scores):
    row_at, col_at = iotas((WIDTH, WIDTH))
    top, left = row_at < HALF, col_at < HALF
    below = (row_at >= HALF) & (left | (row_at >= col_at))
    above = top & (row_at > col_at)
    count = packets.shape[0]
    halves, shifts, offsets, centres = [], [], [], []
    for k in range(count):
        both, flipped = unfolded(packets[k, :HALF])
        diag, shift, centre, offset = (packets[k, HALF + n : HALF + n + 1] for n in range(4))
        whiten = jnp.where(below, both, jnp.where(above, flipped, 0.0))
        whiten = jnp.where(top & (row_at == col_at), diag, whiten)
        halves.append(whiten.astype(jnp.bfloat16))
        shifts.append(jnp.broadcast_to(shift, (WIDTH, WIDTH)).T)
        offsets.append(offset)
        centres.append(centre)
    halves = jnp.concatenate(halves, axis=0)
    offsets = jnp.concatenate(offsets, axis=0)
    offsets = jnp.concatenate([offsets, offsets], axis=1)
    centres = jnp.concatenate(centres, axis=0)
    for block in range(turned.shape[0]):
        proj = matmul(halves, turned[block])
        quads = []
        for k in range(count):
            shift = jnp.concatenate([shifts[k], shifts[k]], axis=1)
            off = proj[k * WIDTH : (k + 1) * WIDTH] - shift
            quads.append(jnp.sum(off * off, axis=0, keepdims=True))
        scores[block, :, :CELLS] = offsets - 0.5 * jnp.concatenate(quads, axis=0)
        scores[block, :, CELLS:] = centres


def likely_kernel(core, tile, part, mask, total, state, resp, near, far, means, totals):
    values = part[:, :CELLS]
    row = iotas((part.shape[0], WIDTH))[0]
    for n in range(2):
        own = jnp.where(row == 2 * tile[0] + n, part[:, CELLS:], 0.0)
        means[n : n + 1] = jnp.sum(own, axis=0, keepdims=True)
    tissue_f = mask[mask.shape[0] - 1 :]
    top = jnp.max(values, axis=0, keepdims=True)
    expon = jnp.exp(values - top)
    weight = jnp.sum(expon, axis=0, keepdims=True)
    first = expon / weight * tissue_f
    keep(values, first, tissue_f, state)
    put(core[0], first, resp, near, far)
    lse = jnp.sum((top + jnp.log(weight)) * tissue_f, axis=1, keepdims=True)
    cells = jnp.sum(tissue_f, axis=1, keepdims=True)
    lane = iotas((1, WIDTH))[1]
    result = jnp.where(lane == 0, lse, jnp.where(lane == 1, cells, total[...]))
    for n in range(totals.shape[0]):
        totals[n] = jnp.broadcast_to(result, totals.shape[1:])


def swap_all(value, axes):
    return lax.all_to_all(value, axes, 0, 0, tiled=True)


def swap_lines(value, groups):
    return lax.all_to_all(value, PLANE, 0, 0, axis_index_groups=groups, tiled=True)


def shards(embed, tissue, whiten0, means0, weights0):
    count = whiten0.shape[0]
    f32 = jnp.float32
    flat = embed.reshape(CELLS, WIDTH)
    core = lax.axis_index("core").reshape(1)
    tile = lax.axis_index(TILE).reshape(1)
    resp_shapes = [((count, CELLS), f32), ((count, WIDTH), f32), ((count, WIDTH), f32)]
    state_shape = ((2 * count + 8, CELLS), f32)

    before, resp, near, far, spread = start(
        core, weights0.reshape(1, count), flat, tissue.reshape(2, WIDTH), means0, whiten0
    )
    shared = swap_all(spread, BRICK)
    kept_shape = ((count + 8, CELLS), f32)
    resp, near, far, kept = call(
        early_kernel, resp_shapes + [kept_shape], core, before, *halos(resp, near, far), scalars=1
    )
    resp, near, far, shared = lax.optimization_barrier((resp, near, far, shared))
    (resp,) = call(
        later_kernel, resp_shapes[:1], core, kept, resp, *halos(resp, near, far), scalars=1
    )

    part = swap_all(resp.reshape(8, 8, CELLS), BRICK)
    packets, turned, total = call(
        moments_kernel,
        [((8, PACKET, WIDTH), f32), ((8, WIDTH, CELLS), jnp.bfloat16), ((1, WIDTH), f32)],
        part, shared, flops=1 << 30,
    )
    (packets,) = call(gather_kernel, [((8, PACKET, WIDTH), f32)], swap_lines(packets, NEAR))
    packets = swap_lines(packets, FAR)
    (packets,) = call(factor_kernel, [((8, PACKET, WIDTH), f32)], packets, flops=1 << 27)
    packets = swap_lines(packets, NEAR)
    (part,) = call(
        second_kernel, [((8, 8, CELLS + WIDTH), f32)], packets, turned, flops=1 << 29
    )
    part = swap_all(part, BRICK).reshape(count, CELLS + WIDTH)

    sizes = [lax.axis_size(axes) for axes in ROUND]
    state, resp, near, far, means_out, totals = call(
        likely_kernel,
        [state_shape] + resp_shapes + [((2, WIDTH), f32), ((sizes[0], 16, WIDTH), f32)],
        core, tile, part, kept, total, scalars=2,
    )
    totals = swap_all(totals, ROUND[0])
    resp, near, far, totals = call(
        middle_kernel, resp_shapes + [((sizes[1], 8, WIDTH), f32)],
        core, state, *halos(resp, near, far), totals, scalars=1,
    )
    totals = swap_all(totals, ROUND[1])
    sides = halos(resp, near, far)
    resp_final, score = pl.pallas_call(
        last_kernel,
        out_shape=[
            jax.ShapeDtypeStruct((count, 2, WIDTH), f32), jax.ShapeDtypeStruct((1, 1), f32)
        ],
        in_specs=[SMEM] + [VMEM] * 7,
        out_specs=[VMEM, SMEM],
        compiler_params=PARAMS,
    )(core, state, resp, *sides, totals)
    return (resp_final.reshape(count, 1, 2, WIDTH), means_out, score.reshape(()))


def solution(mesh):
    bits = Mesh(mesh.devices.reshape((2,) * 9), SLAB + TILE)
    in_specs = (P(SLAB, TILE, None, None), P(SLAB, TILE, None), P(), P(), P())
    out_specs = (P(None, SLAB, TILE, None), P(TILE, None), P())
    return jax.shard_map(shards, mesh=bits, in_specs=in_specs, out_specs=out_specs, check_vma=False)
```

```python
import jax
import jax.numpy as jnp
from jax import lax
from jax.experimental import pallas as pl
from jax.experimental.pallas import tpu as pltpu
from jax.sharding import Mesh
from jax.sharding import PartitionSpec as P

SWEEPS = 2
BETA_POTTS = 1.0
COV_RIDGE = 0.01

SLAB = ("x1", "x0", "z2", "z1")
TILE = ("z0", "y2", "y1", "y0", "core")
BRICK = ("x1", "x0", "core")
PLANE = ("z2", "z1", "z0", "y2", "y1", "y0", "core")
ALONG_Y = [[[z * 16 + y * 2 + core for y in range(8)] for z in range(8)] for core in range(2)]
ALONG_Z = [[[z * 16 + y * 2 + core for z in range(8)] for y in range(8)] for core in range(2)]
NEAR = ALONG_Y[0] + ALONG_Z[1]
FAR = ALONG_Z[0] + ALONG_Y[1]

WIDTH = 128
CELLS = 256
DEVICES = 512
HALF = 64
PARTS = CELLS + WIDTH
PACKET = HALF + 8
VMEM = pl.BlockSpec(memory_space=pltpu.VMEM)
SMEM = pl.BlockSpec(memory_space=pltpu.SMEM)
HBM = pl.BlockSpec(memory_space=pl.ANY)
PARAMS = pltpu.CompilerParams(vmem_limit_bytes=40 * 1024 * 1024)


def call(kernel, shapes, *args, scalars=0, flops=1 << 20):
    out = [jax.ShapeDtypeStruct(shape, kind) for shape, kind in shapes]
    return pl.pallas_call(
        kernel,
        out_shape=out,
        in_specs=[SMEM] * scalars + [VMEM] * (len(args) - scalars),
        out_specs=[VMEM] * len(out),
        compiler_params=PARAMS,
        cost_estimate=pl.CostEstimate(flops=flops, bytes_accessed=1 << 20, transcendentals=0),
    )(*args)


def iotas(shape):
    return (
        lax.broadcasted_iota(jnp.int32, shape, 0),
        lax.broadcasted_iota(jnp.int32, shape, 1),
    )


def matmul(lhs, rhs, dims=((1,), (0,))):
    return lax.dot_general(lhs, rhs, (dims, ((), ())), preferred_element_type=jnp.float32)


def normalise(scores):
    top = jnp.max(scores, axis=0, keepdims=True)
    expon = jnp.exp(scores - top)
    return expon / jnp.sum(expon, axis=0, keepdims=True)


def keep(scores, resp, mask, state):
    count = scores.shape[0]
    state[:count] = scores
    state[count : 2 * count] = resp
    state[2 * count :] = jnp.broadcast_to(mask, (state.shape[0] - 2 * count, CELLS))


def put(core, resp, resp_ref, near_ref, far_ref):
    first, last = resp[:, :WIDTH], resp[:, WIDTH:]
    resp_ref[...] = resp
    near_ref[...] = jnp.where(core == 0, last, first)
    far_ref[...] = jnp.where(core == 0, first, last)


CHUNK = 16


def start_kernel(
    core, weights, flat, tissue, means, whiten,
    state, resp, near, far, spread,
    weights_in, flat_in, tissue_in, means_in, whiten_in, diag, sems,
):
    count = whiten.shape[0]
    small = zip((flat, means, tissue, weights), (flat_in, means_in, tissue_in, weights_in))
    copies = [pltpu.make_async_copy(src, dst, sems.at[n]) for n, (src, dst) in enumerate(small)]
    blocks = [
        pltpu.make_async_copy(
            whiten.at[pl.ds(begin, CHUNK)],
            whiten_in.at[pl.ds(begin, CHUNK)],
            sems.at[4 + begin // CHUNK],
        )
        for begin in range(0, count, CHUNK)
    ]
    for copy in copies + blocks:
        copy.start()
    row_at, col_at = iotas((WIDTH, WIDTH))
    copies[0].wait()
    full = flat_in[...].astype(jnp.float32)
    cells = full.T.astype(jnp.bfloat16)
    for n in range(spread.shape[0]):
        spread[n, :CELLS] = full
    for copy in copies[1:]:
        copy.wait()
    tissue_f = tissue_in[...].astype(jnp.float32)
    rows = jnp.concatenate([tissue_f, jnp.zeros((6, WIDTH), jnp.float32)], axis=0)
    for n in range(spread.shape[0]):
        spread[n, CELLS:] = rows
    for n, block in enumerate(blocks):
        block.wait()
        for own in range(n * CHUNK, (n + 1) * CHUNK):
            matrix = whiten_in[own]
            full = matrix.astype(jnp.float32)
            shift = jnp.sum(full * means_in[own : own + 1], axis=1, keepdims=True)
            proj = matmul(matrix, cells) - shift
            state[own : own + 1] = jnp.sum(proj * proj, axis=0, keepdims=True)
            diag[own : own + 1] = jnp.sum(
                jnp.where(row_at == col_at, full, 0.0), axis=0, keepdims=True
            )
    prior = weights_in[...]
    prior = jnp.log(prior / jnp.sum(prior, axis=1, keepdims=True))
    row_at, col_at = iotas((count, count))
    prior = jnp.where(row_at == col_at, jnp.broadcast_to(prior, (count, count)), 0.0)
    offset = jnp.sum(prior, axis=1, keepdims=True) + jnp.sum(
        jnp.log(diag[...]), axis=1, keepdims=True
    )
    result = offset - 0.5 * state[:count]
    tissue_f = jnp.concatenate([tissue_f[:1], tissue_f[1:]], axis=1)
    first = normalise(result) * tissue_f
    keep(result, first, tissue_f, state)
    put(core[0], first, resp, near, far)


def start(core, weights, flat, tissue, means, whiten):
    count = whiten.shape[0]
    f32 = jnp.float32
    shapes = [(2 * count + 8, CELLS), (count, CELLS), (count, WIDTH), (count, WIDTH)]
    shapes += [(8, CELLS + 8, WIDTH)]
    return pl.pallas_call(
        start_kernel,
        out_shape=[jax.ShapeDtypeStruct(shape, f32) for shape in shapes],
        in_specs=[SMEM] + [HBM] * 5,
        out_specs=[VMEM] * len(shapes),
        scratch_shapes=[
            pltpu.VMEM(weights.shape, f32),
            pltpu.VMEM(flat.shape, flat.dtype),
            pltpu.VMEM(tissue.shape, tissue.dtype),
            pltpu.VMEM(means.shape, f32),
            pltpu.VMEM(whiten.shape, whiten.dtype),
            pltpu.VMEM((count, WIDTH), f32),
            pltpu.SemaphoreType.DMA((4 + count // CHUNK,)),
        ],
        compiler_params=pltpu.CompilerParams(vmem_limit_bytes=58 * 1024 * 1024),
        cost_estimate=pl.CostEstimate(flops=1 << 29, bytes_accessed=1 << 21, transcendentals=0),
    )(core, weights, flat, tissue, means, whiten)


def swept(core, state, resp, slab_even, slab_odd, far_in, near_in):
    count = resp.shape[0]
    lane = iotas((count, WIDTH))[1]
    rows = (resp[:, :WIDTH], resp[:, WIDTH:])
    below = jnp.where(core[0] == 0, far_in[...], near_in[...])
    above = jnp.where(core[0] == 0, near_in[...], far_in[...])
    fields = []
    for row, others in zip(rows, (below + rows[1], rows[0] + above)):
        after = jnp.where(lane < WIDTH - 1, pltpu.roll(row, WIDTH - 1, 1), 0.0)
        before = jnp.where(lane > 0, pltpu.roll(row, 1, 1), 0.0)
        fields.append(others + after + before)
    field = jnp.concatenate(fields, axis=1) + slab_even[...] + slab_odd[...]
    scores, mask = state[:count], state[state.shape[0] - 1 :]
    return normalise(scores + BETA_POTTS * field) * mask


def first_kernel(core, state, slab_even, slab_odd, far_in, near_in, out, near, far):
    count = out.shape[0]
    resp = state[count : 2 * count]
    put(core[0], swept(core, state, resp, slab_even, slab_odd, far_in, near_in), out, near, far)


def early_kernel(core, state, slab_even, slab_odd, far_in, near_in, out, near, far, kept):
    count = out.shape[0]
    kept[:count] = state[:count]
    kept[count:] = state[2 * count :]
    first_kernel(core, state, slab_even, slab_odd, far_in, near_in, out, near, far)


def middle_kernel(
    core, state, slab_even, slab_odd, far_in, near_in, totals, out, near, far, sums
):
    total = totals[0]
    for n in range(1, totals.shape[0]):
        total = total + totals[n]
    for n in range(sums.shape[0]):
        sums[n] = total[: sums.shape[1]]
    first_kernel(core, state, slab_even, slab_odd, far_in, near_in, out, near, far)


def later_kernel(core, state, resp, slab_even, slab_odd, far_in, near_in, out):
    out[...] = swept(core, state, resp[...], slab_even, slab_odd, far_in, near_in)


def last_kernel(core, state, resp, slab_even, slab_odd, far_in, near_in, totals, out, score):
    result = swept(core, state, resp[...], slab_even, slab_odd, far_in, near_in)
    out[:, 0, :] = result[:, :WIDTH]
    out[:, 1, :] = result[:, WIDTH:]
    total = totals[0]
    for n in range(1, totals.shape[0]):
        total = total + totals[n]
    total = total[:1]
    lane = iotas((1, WIDTH))[1]
    lse = jnp.sum(jnp.where(lane == 0, total, 0.0))
    level = jnp.sum(jnp.where(lane == 1, jnp.log(total), 0.0))
    cells = jnp.sum(jnp.where(lane == 1, total, 0.0))
    score[0, 0] = (lse - cells * level) / (CELLS * DEVICES)


def swapped(part, axes, begin):
    count = lax.axis_size(axes)
    pairs = [(i, i + 1) for i in range(begin, count - 1, 2)]
    return lax.ppermute(part, axes, pairs + [(j, i) for i, j in pairs])


def halos(resp, near, far):
    return (
        swapped(resp, SLAB, 0), swapped(resp, SLAB, 1), swapped(far, TILE, 1), swapped(near, TILE, 0)
    )


def moments_kernel(resp, shared, packet, turned, cover):
    blocks, count = resp.shape[:2]
    row_at, col_at = iotas((WIDTH, WIDTH))
    ones = jnp.ones((CELLS, WIDTH), jnp.bfloat16)
    acc = [jnp.zeros((WIDTH, 2 * WIDTH), jnp.float32) for _ in range(count)]
    for block in range(blocks):
        cells, weight = shared[block, :CELLS], resp[block]
        tissue_f = shared[block, CELLS:]
        cover[block : block + 1] = jnp.concatenate([tissue_f[:1], tissue_f[1:2]], axis=1)
        flipped = cells.T
        turned[block] = flipped.astype(jnp.bfloat16)
        wide = jnp.concatenate([cells.astype(jnp.bfloat16), ones], axis=1)
        for k in range(count):
            weighted = (flipped * weight[k : k + 1]).astype(jnp.bfloat16)
            acc[k] = acc[k] + matmul(weighted, wide)
    firsts = jnp.zeros((WIDTH, WIDTH), jnp.float32)
    for k in range(count):
        firsts = jnp.where(col_at == k, acc[k][:, WIDTH:], firsts)
    firsts = firsts.T
    counts = jnp.sum(jnp.sum(resp[...], axis=0), axis=1, keepdims=True)
    counts = jnp.broadcast_to(counts, (count, WIDTH))
    fold_row, fold_col = iotas((HALF, WIDTH))
    for k in range(count):
        sym = acc[k][:, :WIDTH]
        sym = sym + sym.T
        low = (fold_col < HALF) | (fold_row > fold_col - HALF)
        packet[k, :HALF] = jnp.where(low, sym[HALF:], pltpu.roll(sym[:HALF], HALF, 1))
        diag = jnp.sum(jnp.where(row_at == col_at, sym, 0.0), axis=0, keepdims=True)
        packet[k, HALF:] = jnp.concatenate(
            [diag, firsts[k : k + 1], counts[k : k + 1], jnp.zeros((5, WIDTH), jnp.float32)],
            axis=0,
        )


def gather_kernel(packets, out):
    total = jnp.sum(packets[...], axis=0)
    for k in range(out.shape[0]):
        out[k] = total


def split(value):
    high = value.astype(jnp.bfloat16).astype(jnp.float32)
    rest = value - high
    middle = rest.astype(jnp.bfloat16).astype(jnp.float32)
    return high, middle, rest - middle


STEP = 16


def whiten_chain(cov):
    row_at, col_at = iotas((WIDTH, WIDTH))
    wide = (STEP, 2 * WIDTH)
    rest = jnp.concatenate([cov, jnp.where(row_at == col_at, 1.0, 0.0)], axis=1)
    sub = lax.broadcasted_iota(jnp.int32, (STEP, WIDTH), 0)
    done, scales = [], []
    for begin in range(0, WIDTH, STEP):
        panel = rest[:STEP]
        cols = [
            jnp.broadcast_to(panel[:, begin + j : begin + j + 1], (STEP, WIDTH))
            for j in range(STEP)
        ]
        scale = jnp.broadcast_to(cols[0][:1], (STEP, WIDTH))
        for j in range(STEP - 1):
            inverse = lax.rsqrt(cols[j][j : j + 1])
            inverse = inverse * inverse
            mult = jnp.where(sub > j, cols[j] * inverse, 0.0)
            for l in range(j + 1, STEP):
                cols[l] = cols[l] - mult * jnp.broadcast_to(cols[l][j : j + 1], (STEP, WIDTH))
            both = jnp.concatenate([mult, mult], axis=1)
            panel = panel - both * jnp.broadcast_to(panel[j : j + 1], wide)
            pivot = jnp.broadcast_to(cols[j + 1][j + 1 : j + 2], (STEP, WIDTH))
            scale = jnp.where(sub > j, pivot, scale)
        root = lax.rsqrt(scale)
        panel = panel * jnp.concatenate([root, root], axis=1)
        scales.append(scale)
        done.append(panel[:, WIDTH:])
        if begin + STEP < WIDTH:
            high, middle, low = split(panel)
            right = jnp.concatenate([high, middle, low, high, middle, high], axis=0)
            high, middle, low = (part[:, :WIDTH] for part in (high, middle, low))
            left = jnp.concatenate([high, high, high, middle, middle, low], axis=0)
            update = matmul(left.astype(jnp.bfloat16), right.astype(jnp.bfloat16), ((0,), (0,)))
            rest = rest[STEP:] - update[begin + STEP :]
    logdet = -0.5 * jnp.sum(jnp.log(jnp.concatenate(scales, axis=0)), axis=0, keepdims=True)
    return jnp.concatenate(done, axis=0), logdet


def unfolded(fold):
    both = jnp.concatenate([pltpu.roll(fold, HALF, 1), fold], axis=0)
    return both, both.T


def factor_kernel(packets, out):
    row_at, col_at = iotas((WIDTH, WIDTH))
    packet = jnp.sum(packets[...], axis=0)
    both, turned = unfolded(packet[:HALF])
    diag, first, counts = (packet[HALF + n : HALF + n + 1] for n in range(3))
    left = col_at < HALF
    kept = (left & (row_at <= col_at)) | ((row_at >= HALF) & (left | (row_at > col_at)))
    sym = jnp.where(row_at == col_at, diag, jnp.where(kept, both, turned))
    centre = first / counts
    tall = jnp.broadcast_to(centre, (WIDTH, WIDTH))
    cov = 0.5 * sym / counts - tall.T * tall
    cov = jnp.where(row_at == col_at, cov + COV_RIDGE, cov)
    whiten, logdet = whiten_chain(cov)
    shift = jnp.sum(whiten * tall, axis=1, keepdims=True)
    shift = jnp.broadcast_to(shift, (WIDTH, WIDTH)).T[:1]
    offset = jnp.log(counts) + logdet
    diag = jnp.sum(jnp.where(row_at == col_at, whiten, 0.0), axis=0, keepdims=True)
    fold_row, fold_col = iotas((HALF, WIDTH))
    low = (fold_col < HALF) | (fold_row >= fold_col - HALF)
    fold = jnp.where(low, whiten[HALF:], pltpu.roll(whiten.T[:HALF], HALF, 1))
    zeros = jnp.zeros((4, WIDTH), jnp.float32)
    result = jnp.concatenate([fold, diag, shift, centre, offset, zeros], axis=0)
    for k in range(out.shape[0]):
        out[k] = result


def second_kernel(packets, turned, scores):
    row_at, col_at = iotas((WIDTH, WIDTH))
    top, left = row_at < HALF, col_at < HALF
    below = (row_at >= HALF) & (left | (row_at >= col_at))
    above = top & (row_at > col_at)
    count = packets.shape[0]
    halves, shifts, offsets, centres = [], [], [], []
    for k in range(count):
        both, flipped = unfolded(packets[k, :HALF])
        diag, shift, centre, offset = (packets[k, HALF + n : HALF + n + 1] for n in range(4))
        whiten = jnp.where(below, both, jnp.where(above, flipped, 0.0))
        whiten = jnp.where(top & (row_at == col_at), diag, whiten)
        halves.append(whiten.astype(jnp.bfloat16))
        shifts.append(jnp.broadcast_to(shift, (WIDTH, WIDTH)).T)
        offsets.append(offset)
        centres.append(centre)
    halves = jnp.concatenate(halves, axis=0)
    offsets = jnp.concatenate(offsets, axis=0)
    offsets = jnp.concatenate([offsets, offsets], axis=1)
    centres = jnp.concatenate(centres, axis=0)
    tops, weights = [], []
    for block in range(turned.shape[0]):
        proj = matmul(halves, turned[block])
        quads = []
        for k in range(count):
            shift = jnp.concatenate([shifts[k], shifts[k]], axis=1)
            off = proj[k * WIDTH : (k + 1) * WIDTH] - shift
            quads.append(jnp.sum(off * off, axis=0, keepdims=True))
        values = offsets - 0.5 * jnp.concatenate(quads, axis=0)
        scores[block, :, :CELLS] = values
        scores[block, :, CELLS:PARTS] = centres
        tops.append(jnp.max(values, axis=0, keepdims=True))
        weights.append(jnp.sum(jnp.exp(values - tops[-1]), axis=0, keepdims=True))
    tops = jnp.concatenate(tops, axis=0)
    weights = jnp.concatenate(weights, axis=0)
    for block in range(turned.shape[0]):
        scores[block, :, PARTS : PARTS + CELLS] = tops
        scores[block, :, PARTS + CELLS :] = weights


def likely_kernel(core, tile, part, mask, cover, state, resp, near, far, means, totals):
    values = part[:, :CELLS]
    count = values.shape[0]
    row = iotas((count, WIDTH))[0]
    for n in range(2):
        own = jnp.where(row == 2 * tile[0] + n, part[:, CELLS:PARTS], 0.0)
        means[n : n + 1] = jnp.sum(own, axis=0, keepdims=True)
    tissue_f = mask[mask.shape[0] - 1 :]
    first = normalise(values) * tissue_f
    keep(values, first, tissue_f, state)
    put(core[0], first, resp, near, far)
    parts = [part[n : n + 8, PARTS:] for n in range(0, count, 8)]
    top = parts[0][:, :CELLS]
    for one in parts[1:]:
        top = jnp.maximum(top, one[:, :CELLS])
    weight = jnp.zeros(top.shape, jnp.float32)
    for one in parts:
        weight = weight + one[:, CELLS:] * jnp.exp(one[:, :CELLS] - top)
    lse = jnp.sum((top + jnp.log(weight)) * cover[...], axis=0, keepdims=True)
    lse = jnp.sum(lse, axis=1, keepdims=True)
    cells = jnp.sum(jnp.sum(cover[...], axis=0, keepdims=True), axis=1, keepdims=True)
    lane = iotas((1, WIDTH))[1]
    result = jnp.where(lane == 0, lse, cells)
    for n in range(totals.shape[0]):
        totals[n] = jnp.broadcast_to(result, totals.shape[1:])


def swap_all(value, axes):
    return lax.all_to_all(value, axes, 0, 0, tiled=True)


def swap_lines(value, groups):
    return lax.all_to_all(value, PLANE, 0, 0, axis_index_groups=groups, tiled=True)


def shards(embed, tissue, whiten0, means0, weights0):
    count = whiten0.shape[0]
    f32 = jnp.float32
    flat = embed.reshape(CELLS, WIDTH)
    core = lax.axis_index("core").reshape(1)
    tile = lax.axis_index(TILE).reshape(1)
    resp_shapes = [((count, CELLS), f32), ((count, WIDTH), f32), ((count, WIDTH), f32)]
    state_shape = ((2 * count + 8, CELLS), f32)

    before, resp, near, far, spread = start(
        core, weights0.reshape(1, count), flat, tissue.reshape(2, WIDTH), means0, whiten0
    )
    shared = swap_all(spread, BRICK)
    kept_shape = ((count + 8, CELLS), f32)
    resp, near, far, kept = call(
        early_kernel, resp_shapes + [kept_shape], core, before, *halos(resp, near, far), scalars=1
    )
    resp, near, far, shared = lax.optimization_barrier((resp, near, far, shared))
    (resp,) = call(
        later_kernel, resp_shapes[:1], core, kept, resp, *halos(resp, near, far), scalars=1
    )

    part = swap_all(resp.reshape(8, 8, CELLS), BRICK)
    packets, turned, cover = call(
        moments_kernel,
        [((8, PACKET, WIDTH), f32), ((8, WIDTH, CELLS), jnp.bfloat16), ((8, CELLS), f32)],
        part, shared, flops=1 << 30,
    )
    (packets,) = call(gather_kernel, [((8, PACKET, WIDTH), f32)], swap_lines(packets, NEAR))
    packets = swap_lines(packets, FAR)
    (packets,) = call(factor_kernel, [((8, PACKET, WIDTH), f32)], packets, flops=1 << 27)
    packets = swap_lines(packets, NEAR)
    (part,) = call(
        second_kernel, [((8, 8, PARTS + 2 * CELLS), f32)], packets, turned, flops=1 << 29
    )
    part = swap_all(part, BRICK).reshape(count, PARTS + 2 * CELLS)

    sum_shape = ((8, 32, WIDTH), f32)
    state, resp, near, far, means_out, totals = call(
        likely_kernel,
        [state_shape] + resp_shapes + [((2, WIDTH), f32), sum_shape],
        core, tile, part, kept, cover, scalars=2,
    )
    totals = swap_lines(totals, NEAR)
    resp, near, far, totals = call(
        middle_kernel, resp_shapes + [sum_shape],
        core, state, *halos(resp, near, far), totals, scalars=1,
    )
    totals = swap_lines(totals, FAR)
    sides = halos(resp, near, far)
    resp_final, score = pl.pallas_call(
        last_kernel,
        out_shape=[
            jax.ShapeDtypeStruct((count, 2, WIDTH), f32), jax.ShapeDtypeStruct((1, 1), f32)
        ],
        in_specs=[SMEM] + [VMEM] * 7,
        out_specs=[VMEM, SMEM],
        compiler_params=PARAMS,
    )(core, state, resp, *sides, totals)
    return (resp_final.reshape(count, 1, 2, WIDTH), means_out, score.reshape(()))


def solution(mesh):
    bits = Mesh(mesh.devices.reshape((2,) * 9), SLAB + TILE)
    in_specs = (P(SLAB, TILE, None, None), P(SLAB, TILE, None), P(), P(), P())
    out_specs = (P(None, SLAB, TILE, None), P(TILE, None), P())
    return jax.shard_map(shards, mesh=bits, in_specs=in_specs, out_specs=out_specs, check_vma=False)
```

```python
import jax
import jax.numpy as jnp
from jax import lax
from jax.experimental import pallas as pl
from jax.experimental.pallas import tpu as pltpu
from jax.sharding import Mesh
from jax.sharding import PartitionSpec as P

SWEEPS = 2
BETA_POTTS = 1.0
COV_RIDGE = 0.01

SLAB = ("x1", "x0", "z2", "z1")
TILE = ("z0", "y2", "y1", "y0", "core")
BRICK = ("x1", "x0", "core")
PLANE = ("z2", "z1", "z0", "y2", "y1", "y0", "core")
ALONG_Y = [[[z * 16 + y * 2 + core for y in range(8)] for z in range(8)] for core in range(2)]
ALONG_Z = [[[z * 16 + y * 2 + core for z in range(8)] for y in range(8)] for core in range(2)]
NEAR = ALONG_Y[0] + ALONG_Z[1]
FAR = ALONG_Z[0] + ALONG_Y[1]
ROUND = (("y2", "y1", "y0", "core"), ("x1", "x0", "z2", "z1", "z0"))

WIDTH = 128
CELLS = 256
DEVICES = 512
HALF = 64
PACKET = HALF + 8
VMEM = pl.BlockSpec(memory_space=pltpu.VMEM)
SMEM = pl.BlockSpec(memory_space=pltpu.SMEM)
HBM = pl.BlockSpec(memory_space=pl.ANY)
PARAMS = pltpu.CompilerParams(vmem_limit_bytes=40 * 1024 * 1024)


def call(kernel, shapes, *args, scalars=0, flops=1 << 20):
    out = [jax.ShapeDtypeStruct(shape, kind) for shape, kind in shapes]
    return pl.pallas_call(
        kernel,
        out_shape=out,
        in_specs=[SMEM] * scalars + [VMEM] * (len(args) - scalars),
        out_specs=[VMEM] * len(out),
        compiler_params=PARAMS,
        cost_estimate=pl.CostEstimate(flops=flops, bytes_accessed=1 << 20, transcendentals=0),
    )(*args)


def iotas(shape):
    return (
        lax.broadcasted_iota(jnp.int32, shape, 0),
        lax.broadcasted_iota(jnp.int32, shape, 1),
    )


def matmul(lhs, rhs, dims=((1,), (0,))):
    return lax.dot_general(lhs, rhs, (dims, ((), ())), preferred_element_type=jnp.float32)


def normalise(scores):
    top = jnp.max(scores, axis=0, keepdims=True)
    expon = jnp.exp(scores - top)
    return expon / jnp.sum(expon, axis=0, keepdims=True)


def keep(scores, resp, mask, state):
    count = scores.shape[0]
    state[:count] = scores
    state[count : 2 * count] = resp
    state[2 * count :] = jnp.broadcast_to(mask, (state.shape[0] - 2 * count, CELLS))


def put(core, resp, resp_ref, near_ref, far_ref):
    first, last = resp[:, :WIDTH], resp[:, WIDTH:]
    resp_ref[...] = resp
    near_ref[...] = jnp.where(core == 0, last, first)
    far_ref[...] = jnp.where(core == 0, first, last)


CHUNK = 16


def start_kernel(
    core, weights, flat, tissue, means, whiten,
    state, resp, near, far, spread,
    weights_in, flat_in, tissue_in, means_in, whiten_in, diag, sems,
):
    count = whiten.shape[0]
    small = zip((flat, means, tissue, weights), (flat_in, means_in, tissue_in, weights_in))
    copies = [pltpu.make_async_copy(src, dst, sems.at[n]) for n, (src, dst) in enumerate(small)]
    blocks = [
        pltpu.make_async_copy(
            whiten.at[pl.ds(begin, CHUNK)],
            whiten_in.at[pl.ds(begin, CHUNK)],
            sems.at[4 + begin // CHUNK],
        )
        for begin in range(0, count, CHUNK)
    ]
    for copy in copies + blocks:
        copy.start()
    row_at, col_at = iotas((WIDTH, WIDTH))
    copies[0].wait()
    full = flat_in[...].astype(jnp.float32)
    cells = full.T.astype(jnp.bfloat16)
    for n in range(spread.shape[0]):
        spread[n] = full
    for copy in copies[1:]:
        copy.wait()
    for n, block in enumerate(blocks):
        block.wait()
        for own in range(n * CHUNK, (n + 1) * CHUNK):
            matrix = whiten_in[own]
            full = matrix.astype(jnp.float32)
            shift = jnp.sum(full * means_in[own : own + 1], axis=1, keepdims=True)
            proj = matmul(matrix, cells) - shift
            state[own : own + 1] = jnp.sum(proj * proj, axis=0, keepdims=True)
            diag[own : own + 1] = jnp.sum(
                jnp.where(row_at == col_at, full, 0.0), axis=0, keepdims=True
            )
    prior = weights_in[...]
    prior = jnp.log(prior / jnp.sum(prior, axis=1, keepdims=True))
    row_at, col_at = iotas((count, count))
    prior = jnp.where(row_at == col_at, jnp.broadcast_to(prior, (count, count)), 0.0)
    offset = jnp.sum(prior, axis=1, keepdims=True) + jnp.sum(
        jnp.log(diag[...]), axis=1, keepdims=True
    )
    result = offset - 0.5 * state[:count]
    tissue_f = tissue_in[...].astype(jnp.float32)
    tissue_f = jnp.concatenate([tissue_f[:1], tissue_f[1:]], axis=1)
    first = normalise(result) * tissue_f
    keep(result, first, tissue_f, state)
    put(core[0], first, resp, near, far)


def start(core, weights, flat, tissue, means, whiten):
    count = whiten.shape[0]
    f32 = jnp.float32
    shapes = [(2 * count + 8, CELLS), (count, CELLS), (count, WIDTH), (count, WIDTH)]
    shapes += [(8, CELLS, WIDTH)]
    return pl.pallas_call(
        start_kernel,
        out_shape=[jax.ShapeDtypeStruct(shape, f32) for shape in shapes],
        in_specs=[SMEM] + [HBM] * 5,
        out_specs=[VMEM] * len(shapes),
        scratch_shapes=[
            pltpu.VMEM(weights.shape, f32),
            pltpu.VMEM(flat.shape, flat.dtype),
            pltpu.VMEM(tissue.shape, tissue.dtype),
            pltpu.VMEM(means.shape, f32),
            pltpu.VMEM(whiten.shape, whiten.dtype),
            pltpu.VMEM((count, WIDTH), f32),
            pltpu.SemaphoreType.DMA((4 + count // CHUNK,)),
        ],
        compiler_params=pltpu.CompilerParams(vmem_limit_bytes=58 * 1024 * 1024),
        cost_estimate=pl.CostEstimate(flops=1 << 29, bytes_accessed=1 << 21, transcendentals=0),
    )(core, weights, flat, tissue, means, whiten)


def swept(core, state, resp, slab_even, slab_odd, far_in, near_in):
    count = resp.shape[0]
    lane = iotas((count, WIDTH))[1]
    rows = (resp[:, :WIDTH], resp[:, WIDTH:])
    below = jnp.where(core[0] == 0, far_in[...], near_in[...])
    above = jnp.where(core[0] == 0, near_in[...], far_in[...])
    fields = []
    for row, others in zip(rows, (below + rows[1], rows[0] + above)):
        after = jnp.where(lane < WIDTH - 1, pltpu.roll(row, WIDTH - 1, 1), 0.0)
        before = jnp.where(lane > 0, pltpu.roll(row, 1, 1), 0.0)
        fields.append(others + after + before)
    field = jnp.concatenate(fields, axis=1) + slab_even[...] + slab_odd[...]
    scores, mask = state[:count], state[state.shape[0] - 1 :]
    return normalise(scores + BETA_POTTS * field) * mask


def first_kernel(core, state, slab_even, slab_odd, far_in, near_in, out, near, far):
    count = out.shape[0]
    resp = state[count : 2 * count]
    put(core[0], swept(core, state, resp, slab_even, slab_odd, far_in, near_in), out, near, far)


def early_kernel(core, state, slab_even, slab_odd, far_in, near_in, out, near, far, kept):
    count = out.shape[0]
    kept[:count] = state[:count]
    kept[count:] = state[2 * count :]
    first_kernel(core, state, slab_even, slab_odd, far_in, near_in, out, near, far)


def middle_kernel(
    core, state, slab_even, slab_odd, far_in, near_in, totals, out, near, far, sums
):
    total = totals[0]
    for n in range(1, totals.shape[0]):
        total = total + totals[n]
    for n in range(sums.shape[0]):
        sums[n] = total[: sums.shape[1]]
    first_kernel(core, state, slab_even, slab_odd, far_in, near_in, out, near, far)


def later_kernel(core, state, resp, slab_even, slab_odd, far_in, near_in, out):
    out[...] = swept(core, state, resp[...], slab_even, slab_odd, far_in, near_in)


def last_kernel(core, state, resp, slab_even, slab_odd, far_in, near_in, totals, out, score):
    result = swept(core, state, resp[...], slab_even, slab_odd, far_in, near_in)
    out[:, 0, :] = result[:, :WIDTH]
    out[:, 1, :] = result[:, WIDTH:]
    total = totals[0]
    for n in range(1, totals.shape[0]):
        total = total + totals[n]
    total = total[:1]
    lane = iotas((1, WIDTH))[1]
    lse = jnp.sum(jnp.where(lane == 0, total, 0.0))
    level = jnp.sum(jnp.where(lane == 2, jnp.log(total), 0.0))
    cells = jnp.sum(jnp.where(lane == 1, total, 0.0))
    score[0, 0] = (lse - cells * level) / (CELLS * DEVICES)


def swapped(part, axes, begin):
    count = lax.axis_size(axes)
    pairs = [(i, i + 1) for i in range(begin, count - 1, 2)]
    return lax.ppermute(part, axes, pairs + [(j, i) for i, j in pairs])


def halos(resp, near, far):
    return (
        swapped(resp, SLAB, 0), swapped(resp, SLAB, 1), swapped(far, TILE, 1), swapped(near, TILE, 0)
    )


def moments_kernel(resp, shared, packet, turned, total):
    blocks, count = resp.shape[:2]
    row_at, col_at = iotas((WIDTH, WIDTH))
    ones = jnp.ones((CELLS, WIDTH), jnp.bfloat16)
    acc = [jnp.zeros((WIDTH, 2 * WIDTH), jnp.float32) for _ in range(count)]
    for block in range(blocks):
        cells, weight = shared[block], resp[block]
        flipped = cells.T
        turned[block] = flipped.astype(jnp.bfloat16)
        wide = jnp.concatenate([cells.astype(jnp.bfloat16), ones], axis=1)
        for k in range(count):
            weighted = (flipped * weight[k : k + 1]).astype(jnp.bfloat16)
            acc[k] = acc[k] + matmul(weighted, wide)
    firsts = jnp.zeros((WIDTH, WIDTH), jnp.float32)
    for k in range(count):
        firsts = jnp.where(col_at == k, acc[k][:, WIDTH:], firsts)
    firsts = firsts.T
    counts = jnp.sum(jnp.sum(resp[...], axis=0), axis=1, keepdims=True)
    counts = jnp.broadcast_to(counts, (count, WIDTH))
    total[...] = jnp.sum(counts, axis=0, keepdims=True)
    fold_row, fold_col = iotas((HALF, WIDTH))
    for k in range(count):
        sym = acc[k][:, :WIDTH]
        sym = sym + sym.T
        low = (fold_col < HALF) | (fold_row > fold_col - HALF)
        packet[k, :HALF] = jnp.where(low, sym[HALF:], pltpu.roll(sym[:HALF], HALF, 1))
        diag = jnp.sum(jnp.where(row_at == col_at, sym, 0.0), axis=0, keepdims=True)
        packet[k, HALF:] = jnp.concatenate(
            [diag, firsts[k : k + 1], counts[k : k + 1], jnp.zeros((5, WIDTH), jnp.float32)],
            axis=0,
        )


def gather_kernel(packets, out):
    total = jnp.sum(packets[...], axis=0)
    for k in range(out.shape[0]):
        out[k] = total


def split(value):
    high = value.astype(jnp.bfloat16).astype(jnp.float32)
    rest = value - high
    middle = rest.astype(jnp.bfloat16).astype(jnp.float32)
    return high, middle, rest - middle


STEP = 16


def whiten_chain(cov):
    row_at, col_at = iotas((WIDTH, WIDTH))
    wide = (STEP, 2 * WIDTH)
    rest = jnp.concatenate([cov, jnp.where(row_at == col_at, 1.0, 0.0)], axis=1)
    sub = lax.broadcasted_iota(jnp.int32, (STEP, WIDTH), 0)
    done, scales = [], []
    for begin in range(0, WIDTH, STEP):
        panel = rest[:STEP]
        cols = [
            jnp.broadcast_to(panel[:, begin + j : begin + j + 1], (STEP, WIDTH))
            for j in range(STEP)
        ]
        scale = jnp.broadcast_to(cols[0][:1], (STEP, WIDTH))
        for j in range(STEP - 1):
            inverse = lax.rsqrt(cols[j][j : j + 1])
            inverse = inverse * inverse
            mult = jnp.where(sub > j, cols[j] * inverse, 0.0)
            for l in range(j + 1, STEP):
                cols[l] = cols[l] - mult * jnp.broadcast_to(cols[l][j : j + 1], (STEP, WIDTH))
            both = jnp.concatenate([mult, mult], axis=1)
            panel = panel - both * jnp.broadcast_to(panel[j : j + 1], wide)
            pivot = jnp.broadcast_to(cols[j + 1][j + 1 : j + 2], (STEP, WIDTH))
            scale = jnp.where(sub > j, pivot, scale)
        root = lax.rsqrt(scale)
        panel = panel * jnp.concatenate([root, root], axis=1)
        scales.append(scale)
        done.append(panel[:, WIDTH:])
        if begin + STEP < WIDTH:
            high, middle, low = split(panel)
            right = jnp.concatenate([high, middle, low, high, middle, high], axis=0)
            high, middle, low = (part[:, :WIDTH] for part in (high, middle, low))
            left = jnp.concatenate([high, high, high, middle, middle, low], axis=0)
            update = matmul(left.astype(jnp.bfloat16), right.astype(jnp.bfloat16), ((0,), (0,)))
            rest = rest[STEP:] - update[begin + STEP :]
    logdet = -0.5 * jnp.sum(jnp.log(jnp.concatenate(scales, axis=0)), axis=0, keepdims=True)
    return jnp.concatenate(done, axis=0), logdet


def unfolded(fold):
    both = jnp.concatenate([pltpu.roll(fold, HALF, 1), fold], axis=0)
    return both, both.T


def factor_kernel(packets, out):
    row_at, col_at = iotas((WIDTH, WIDTH))
    packet = jnp.sum(packets[...], axis=0)
    both, turned = unfolded(packet[:HALF])
    diag, first, counts = (packet[HALF + n : HALF + n + 1] for n in range(3))
    left = col_at < HALF
    kept = (left & (row_at <= col_at)) | ((row_at >= HALF) & (left | (row_at > col_at)))
    sym = jnp.where(row_at == col_at, diag, jnp.where(kept, both, turned))
    centre = first / counts
    tall = jnp.broadcast_to(centre, (WIDTH, WIDTH))
    cov = 0.5 * sym / counts - tall.T * tall
    cov = jnp.where(row_at == col_at, cov + COV_RIDGE, cov)
    whiten, logdet = whiten_chain(cov)
    shift = jnp.sum(whiten * tall, axis=1, keepdims=True)
    shift = jnp.broadcast_to(shift, (WIDTH, WIDTH)).T[:1]
    offset = jnp.log(counts) + logdet
    diag = jnp.sum(jnp.where(row_at == col_at, whiten, 0.0), axis=0, keepdims=True)
    fold_row, fold_col = iotas((HALF, WIDTH))
    low = (fold_col < HALF) | (fold_row >= fold_col - HALF)
    fold = jnp.where(low, whiten[HALF:], pltpu.roll(whiten.T[:HALF], HALF, 1))
    zeros = jnp.zeros((4, WIDTH), jnp.float32)
    result = jnp.concatenate([fold, diag, shift, centre, offset, zeros], axis=0)
    for k in range(out.shape[0]):
        out[k] = result


def second_kernel(packets, turned, scores):
    row_at, col_at = iotas((WIDTH, WIDTH))
    top, left = row_at < HALF, col_at < HALF
    below = (row_at >= HALF) & (left | (row_at >= col_at))
    above = top & (row_at > col_at)
    count = packets.shape[0]
    halves, shifts, offsets, centres = [], [], [], []
    for k in range(count):
        both, flipped = unfolded(packets[k, :HALF])
        diag, shift, centre, offset = (packets[k, HALF + n : HALF + n + 1] for n in range(4))
        whiten = jnp.where(below, both, jnp.where(above, flipped, 0.0))
        whiten = jnp.where(top & (row_at == col_at), diag, whiten)
        halves.append(whiten.astype(jnp.bfloat16))
        shifts.append(jnp.broadcast_to(shift, (WIDTH, WIDTH)).T)
        offsets.append(offset)
        centres.append(centre)
    halves = jnp.concatenate(halves, axis=0)
    offsets = jnp.concatenate(offsets, axis=0)
    offsets = jnp.concatenate([offsets, offsets], axis=1)
    centres = jnp.concatenate(centres, axis=0)
    for block in range(turned.shape[0]):
        proj = matmul(halves, turned[block])
        quads = []
        for k in range(count):
            shift = jnp.concatenate([shifts[k], shifts[k]], axis=1)
            off = proj[k * WIDTH : (k + 1) * WIDTH] - shift
            quads.append(jnp.sum(off * off, axis=0, keepdims=True))
        scores[block, :, :CELLS] = offsets - 0.5 * jnp.concatenate(quads, axis=0)
        scores[block, :, CELLS:] = centres


def likely_kernel(core, tile, part, mask, total, state, resp, near, far, means, totals):
    values = part[:, :CELLS]
    row = iotas((part.shape[0], WIDTH))[0]
    for n in range(2):
        own = jnp.where(row == 2 * tile[0] + n, part[:, CELLS:], 0.0)
        means[n : n + 1] = jnp.sum(own, axis=0, keepdims=True)
    tissue_f = mask[mask.shape[0] - 1 :]
    top = jnp.max(values, axis=0, keepdims=True)
    expon = jnp.exp(values - top)
    weight = jnp.sum(expon, axis=0, keepdims=True)
    first = expon / weight * tissue_f
    keep(values, first, tissue_f, state)
    put(core[0], first, resp, near, far)
    lse = jnp.sum((top + jnp.log(weight)) * tissue_f, axis=1, keepdims=True)
    cells = jnp.sum(tissue_f, axis=1, keepdims=True)
    lane = iotas((1, WIDTH))[1]
    result = jnp.where(lane == 0, lse, jnp.where(lane == 1, cells, total[...]))
    for n in range(totals.shape[0]):
        totals[n] = jnp.broadcast_to(result, totals.shape[1:])


def swap_all(value, axes):
    return lax.all_to_all(value, axes, 0, 0, tiled=True)


def swap_lines(value, groups):
    return lax.all_to_all(value, PLANE, 0, 0, axis_index_groups=groups, tiled=True)


def shards(embed, tissue, whiten0, means0, weights0):
    count = whiten0.shape[0]
    f32 = jnp.float32
    flat = embed.reshape(CELLS, WIDTH)
    core = lax.axis_index("core").reshape(1)
    tile = lax.axis_index(TILE).reshape(1)
    resp_shapes = [((count, CELLS), f32), ((count, WIDTH), f32), ((count, WIDTH), f32)]
    state_shape = ((2 * count + 8, CELLS), f32)

    before, resp, near, far, spread = start(
        core, weights0.reshape(1, count), flat, tissue.reshape(2, WIDTH), means0, whiten0
    )
    shared = swap_all(spread, BRICK)
    kept_shape = ((count + 8, CELLS), f32)
    resp, near, far, kept = call(
        early_kernel, resp_shapes + [kept_shape], core, before, *halos(resp, near, far), scalars=1
    )
    resp, near, far, shared = lax.optimization_barrier((resp, near, far, shared))
    (resp,) = call(
        later_kernel, resp_shapes[:1], core, kept, resp, *halos(resp, near, far), scalars=1
    )

    part = swap_all(resp.reshape(8, 8, CELLS), BRICK)
    packets, turned, total = call(
        moments_kernel,
        [((8, PACKET, WIDTH), f32), ((8, WIDTH, CELLS), jnp.bfloat16), ((1, WIDTH), f32)],
        part, shared, flops=1 << 30,
    )
    (packets,) = call(gather_kernel, [((8, PACKET, WIDTH), f32)], swap_lines(packets, NEAR))
    packets = swap_lines(packets, FAR)
    (packets,) = call(factor_kernel, [((8, PACKET, WIDTH), f32)], packets, flops=1 << 27)
    packets = swap_lines(packets, NEAR)
    (part,) = call(
        second_kernel, [((8, 8, CELLS + WIDTH), f32)], packets, turned, flops=1 << 29
    )
    part = swap_all(part, BRICK).reshape(count, CELLS + WIDTH)

    sizes = [lax.axis_size(axes) for axes in ROUND]
    state, resp, near, far, means_out, totals = call(
        likely_kernel,
        [state_shape] + resp_shapes + [((2, WIDTH), f32), ((sizes[0], 8, WIDTH), f32)],
        core, tile, part, kept, total, scalars=2,
    )
    totals = swap_all(totals, ROUND[0])
    resp, near, far, totals = call(
        middle_kernel, resp_shapes + [((sizes[1], 8, WIDTH), f32)],
        core, state, *halos(resp, near, far), totals, scalars=1,
    )
    totals = swap_all(totals, ROUND[1])
    sides = halos(resp, near, far)
    resp_final, score = pl.pallas_call(
        last_kernel,
        out_shape=[
            jax.ShapeDtypeStruct((count, 2, WIDTH), f32), jax.ShapeDtypeStruct((1, 1), f32)
        ],
        in_specs=[SMEM] + [VMEM] * 7,
        out_specs=[VMEM, SMEM],
        compiler_params=PARAMS,
    )(core, state, resp, *sides, totals)
    return (resp_final.reshape(count, 1, 2, WIDTH), means_out, score.reshape(()))


def solution(mesh):
    bits = Mesh(mesh.devices.reshape((2,) * 9), SLAB + TILE)
    in_specs = (P(SLAB, TILE, None, None), P(SLAB, TILE, None), P(), P(), P())
    out_specs = (P(None, SLAB, TILE, None), P(TILE, None), P())
    return jax.shard_map(shards, mesh=bits, in_specs=in_specs, out_specs=out_specs, check_vma=False)
```
